512 devices in a mesh: ta: 16 (over z), gz: 4 (over x_hi, core), gy: 8 (over y, x_lo).
Axes of the slice: x: 4 (x_hi: 2, x_lo: 2; x = x_hi * 2 + x_lo), y: 4, z: 16, core: 2. Of those that a mesh axis runs over, the one named last changes fastest.
Arguments:
- sources: float32 [4, 2, 4, 3, 32, 8, 1024], P(None, None, None, None, 'ta', 'gz', 'gy'), may hold values from -10 to 10
- gauge_links: float32 [2, 4, 2, 3, 3, 32, 8, 1024], P(None, None, None, None, None, 'ta', 'gz', 'gy'), may hold values from -2.5 to 2.5
Outputs:
- solution: float32 [4, 2, 4, 3, 32, 8, 1024], P(None, None, None, None, 'ta', 'gz', 'gy')
- residual: float32 [4, 2, 4, 3, 32, 8, 1024], P(None, None, None, None, 'ta', 'gz', 'gy')
The draws below stay inside these ranges and needn't reach their ends.
All inputs are finite; a program needn't handle non-finite values.
Results may differ from the reference program's by a relative error of at most 0.0003.
Values sent between devices are 32-bit elements; how exact they have to be, the bound alone decides.
No kernel may reach another device: no remote copies, remote signals or barrier semaphores. Data moves between devices by JAX's collectives and lax.ppermute only.
A program may use at most 128 MiB of HBM per device.

```python
import math
import jax
import jax.numpy as jnp
from jax import lax

SRC = 4
ITERS = 2
XH = 32
NT = 32
NZ = 8
NY = 32
NYX = 1024


def draw_sources(key, part):
    key = jax.random.fold_in(key, 5)
    common_key = jax.random.fold_in(key, 1)
    own_key = jax.random.fold_in(key, 2)
    full_shape = (SRC, 2, 4, 3, NT, NZ, NYX)
    shared_shape = (1, 2, 4, 3, NT, NZ, NYX)
    time_pos = lax.broadcasted_iota(jnp.float32, full_shape, 4) / (NT - 1)
    depth_pos = lax.broadcasted_iota(jnp.float32, full_shape, 5) / (NZ - 1)
    row_pos = (lax.broadcasted_iota(jnp.int32, full_shape, 6) // XH).astype(jnp.float32) / (NY - 1)
    profile = time_pos + depth_pos + row_pos - 1.5
    common = jnp.clip(jax.random.normal(common_key, shared_shape, jnp.float32), -3.0, 3.0)
    own = jnp.clip(jax.random.normal(own_key, full_shape, jnp.float32), -3.0, 3.0)
    values = 0.8 * common + 0.55 * own
    return values * jnp.exp(profile * 0.5 * math.log(3.0))


def block_scale(rng, extent, cuts, smallest, top_value):
    def one(axis_at, blocks):
        steps = jax.random.uniform(jax.random.fold_in(jax.random.fold_in(rng, 6), axis_at), (blocks,), jnp.float32, smallest / len(cuts), top_value / len(cuts))
        return jnp.repeat(jnp.exp(steps), extent[axis_at] // blocks).reshape((-1,) + (1,) * (len(extent) - axis_at - 1))

    factor_of = one(*cuts[0])
    for cut in cuts[1:]:
        factor_of = factor_of * one(*cut)
    return factor_of


def bell_draw(key, extent, scale, limit, cuts=(), kind=jnp.bfloat16):
    drawn = jax.random.normal(key, extent, jnp.float32) * scale
    if len(cuts) > 0:
        drawn = block_scale(key, extent, cuts, -0.22, 0.18) * drawn
    return jnp.clip(drawn, min=-limit, max=limit).astype(kind)


def setup_inputs(seed: int = 0) -> dict:
    streams_of = jax.random.split(jax.random.key(seed), 3)
    sources = draw_sources(jax.random.fold_in(streams_of[2], 71), 0)
    gauge_links = bell_draw(streams_of[1], (2, 4, 2, 3, 3, NT, NZ, NYX), 6 ** -0.5, 2.5, ((5, 16), (6, 4), (7, 8)), jnp.float32)
    return dict(sources=sources, gauge_links=gauge_links)


kappa_square = 0.0196
gamma_columns = ((3, 2, 1, 0), (3, 2, 1, 0), (2, 3, 0, 1), (2, 3, 0, 1))
gamma_phases = (((0, 1), (0, 1), (0, -1), (0, -1)), ((1, 0), (-1, 0), (-1, 0), (1, 0)), ((0, 1), (0, -1), (0, -1), (0, 1)), ((1, 0), (1, 0), (1, 0), (1, 0)))

def phase_times(phase, real_part, imag_part):
    if phase[1] == 0:
        if phase[0] == 1:
            return (real_part, imag_part)
        return (-real_part, -imag_part)
    if phase[1] == 1:
        return (-imag_part, real_part)
    return (imag_part, -real_part)

def project(spinor, direction, hop_sign, row_count):
    real_rows = []
    imag_rows = []
    for spin_row in range(row_count):
        partner = gamma_columns[direction][spin_row]
        moved_real, moved_imag = phase_times(gamma_phases[direction][spin_row], spinor[:, 0, partner], spinor[:, 1, partner])
        if hop_sign > 0:
            real_rows.append(spinor[:, 0, spin_row] + moved_real)
            imag_rows.append(spinor[:, 1, spin_row] + moved_imag)
        else:
            real_rows.append(spinor[:, 0, spin_row] - moved_real)
            imag_rows.append(spinor[:, 1, spin_row] - moved_imag)
    return jnp.stack([jnp.stack(real_rows, 1), jnp.stack(imag_rows, 1)], 1)

def color_times(link, spinor, adjoint):
    link_real = link[0]
    link_imag = link[1]
    if adjoint:
        link_real = jnp.swapaxes(link_real, 0, 1)
        link_imag = -jnp.swapaxes(link_imag, 0, 1)
    spin_real = spinor[:, 0]
    spin_imag = spinor[:, 1]
    out_real = None
    out_imag = None
    for column in range(3):
        entry_real = link_real[:, column]
        entry_imag = link_imag[:, column]
        part_real = entry_real * spin_real[:, :, column:column + 1] - entry_imag * spin_imag[:, :, column:column + 1]
        part_imag = entry_real * spin_imag[:, :, column:column + 1] + entry_imag * spin_real[:, :, column:column + 1]
        if out_real is None:
            out_real, out_imag = (part_real, part_imag)
        else:
            out_real = out_real + part_real
            out_imag = out_imag + part_imag
    return jnp.stack([out_real, out_imag], 1)

def next_cell(values, half_x, cell_x):
    return jnp.where(cell_x == half_x - 1, jnp.roll(values, half_x - 1, -1), jnp.roll(values, -1, -1))

def prior_cell(values, half_x, cell_x):
    return jnp.where(cell_x == 0, jnp.roll(values, 1 - half_x, -1), jnp.roll(values, 1, -1))

def hopping(spinor, gauge_links, out_parity, context):
    row_parity, cell_x, top_sign, bottom_sign = context
    shift_odd = (row_parity + out_parity) % 2
    summed = jnp.zeros_like(spinor)
    for direction in range(4):
        forward = project(spinor, direction, -1, 4)
        backward = color_times(gauge_links[1 - out_parity, direction], project(spinor, direction, 1, 4), True)
        if direction == 0:
            forward = jnp.where(shift_odd == 1, next_cell(forward, XH, cell_x), forward)
            backward = jnp.where(shift_odd == 0, prior_cell(backward, XH, cell_x), backward)
        elif direction == 1:
            forward = jnp.roll(forward, -XH, 6)
            backward = jnp.roll(backward, XH, 6)
        elif direction == 2:
            forward = jnp.roll(forward, -1, 5)
            backward = jnp.roll(backward, 1, 5)
        else:
            forward = jnp.roll(forward, -1, 4) * top_sign
            backward = jnp.roll(backward, 1, 4) * bottom_sign
        summed = summed + color_times(gauge_links[out_parity, direction], forward, False) + backward
    return summed

def wilson_even(spinor, gauge_links, context):
    return spinor - kappa_square * hopping(hopping(spinor, gauge_links, 1, context), gauge_links, 0, context)

def normal_operator(spinor, gauge_links, context):
    gamma_five = jnp.array([1.0, 1.0, -1.0, -1.0], jnp.float32).reshape(1, 1, 4, 1, 1, 1, 1)
    once = gamma_five * wilson_even(spinor, gauge_links, context)
    return gamma_five * wilson_even(once, gauge_links, context)

def contract(left_flat, right_flat):
    return lax.dot_general(left_flat.astype(jnp.float32), right_flat.astype(jnp.float32), (((1,), (1,)), ((), ())), precision=lax.Precision.HIGHEST, preferred_element_type=jnp.float32)

def matmul(left_mat, right_mat):
    return jnp.dot(left_mat.astype(jnp.float32), right_mat.astype(jnp.float32), precision=lax.Precision.HIGHEST, preferred_element_type=jnp.float32)

def gram(left, right):
    source_count = left.shape[0]
    left_real = left[:, 0].reshape(source_count, -1)
    left_imag = left[:, 1].reshape(source_count, -1)
    right_real = right[:, 0].reshape(source_count, -1)
    right_imag = right[:, 1].reshape(source_count, -1)
    real_part = contract(left_real, right_real) + contract(left_imag, right_imag)
    imag_part = contract(left_real, right_imag) - contract(left_imag, right_real)
    return jnp.stack([real_part, imag_part])

def combine(spinors, coeffs):
    source_count = spinors.shape[0]
    real_flat = spinors[:, 0].reshape(source_count, -1)
    imag_flat = spinors[:, 1].reshape(source_count, -1)
    real_new = matmul(coeffs[0].T, real_flat) - matmul(coeffs[1].T, imag_flat)
    imag_new = matmul(coeffs[0].T, imag_flat) + matmul(coeffs[1].T, real_flat)
    return jnp.stack([real_new, imag_new], 1).reshape(spinors.shape)

def cholesky_solve(factor, rhs_rows):
    order_size = factor.shape[0]
    forward_rows = []
    for row_index in range(order_size):
        running = rhs_rows[row_index]
        for col_index in range(row_index):
            running = running - factor[row_index, col_index] * forward_rows[col_index]
        forward_rows.append(running / factor[row_index, row_index])
    back_rows = [None] * order_size
    for row_index in reversed(range(order_size)):
        running = forward_rows[row_index]
        for col_index in range(row_index + 1, order_size):
            running = running - factor[col_index, row_index] * back_rows[col_index]
        back_rows[row_index] = running / factor[row_index, row_index]
    return jnp.stack(back_rows)

def complex_solve(matrix, rhs):
    upper = jnp.concatenate([matrix[0], -matrix[1]], 1)
    lower = jnp.concatenate([matrix[1], matrix[0]], 1)
    embedded = jnp.concatenate([upper, lower], 0)
    embedded = 0.5 * (embedded + embedded.T)
    factor = jnp.linalg.cholesky(embedded)
    stacked = jnp.concatenate([rhs[0], rhs[1]], 0)
    solved = cholesky_solve(factor, stacked)
    half_count = rhs.shape[1]
    return jnp.stack([solved[:half_count], solved[half_count:]])

def reference(sources, gauge_links):
    time_iota = lax.broadcasted_iota(jnp.int32, (NT, NZ, NYX), 0)
    depth_iota = lax.broadcasted_iota(jnp.int32, (NT, NZ, NYX), 1)
    flat_iota = lax.broadcasted_iota(jnp.int32, (NT, NZ, NYX), 2)
    row_parity = (time_iota + depth_iota + flat_iota // XH) % 2
    cell_x = flat_iota % XH
    edge_iota = lax.broadcasted_iota(jnp.int32, (NT, 1, 1), 0)
    top_sign = jnp.where(edge_iota == NT - 1, -1.0, 1.0).astype(jnp.float32)
    bottom_sign = jnp.where(edge_iota == 0, -1.0, 1.0).astype(jnp.float32)
    context = (row_parity, cell_x, top_sign, bottom_sign)

    def apply_one(single):
        return normal_operator(single[None], gauge_links, context)[0]
    solution = jnp.zeros_like(sources)
    residual = sources
    search = sources
    residual_gram = gram(residual, residual)
    for iteration in range(ITERS):
        images = lax.map(apply_one, search)
        curvature = gram(search, images)
        step_coeffs = complex_solve(curvature, residual_gram)
        solution = solution + combine(search, step_coeffs)
        residual = residual - combine(images, step_coeffs)
        if iteration + 1 < ITERS:
            next_gram = gram(residual, residual)
            mixing = complex_solve(residual_gram, next_gram)
            search = residual + combine(search, mixing)
            residual_gram = next_gram
    return (solution, residual)
```

```python
import jax
import jax.numpy as jnp
from jax import lax
from jax.experimental import pallas as pl
from jax.experimental.pallas import tpu as pltpu
from jax.sharding import PartitionSpec as P

SRC = 4
KAPPA_SQUARE = 0.0196
GAMMA_COLUMNS = ((3, 2, 1, 0), (3, 2, 1, 0), (2, 3, 0, 1), (2, 3, 0, 1))
GAMMA_PHASES = (
    ((0, 1), (0, 1), (0, -1), (0, -1)),
    ((1, 0), (-1, 0), (-1, 0), (1, 0)),
    ((0, 1), (0, -1), (0, -1), (0, 1)),
    ((1, 0), (1, 0), (1, 0), (1, 0)),
)
F32 = jnp.float32
TILE = (8, 128)
ROW_OWNER = ((0, 1, 3, 2), (2, 3, 1, 0))
GUARD = 0.005
PIVOT_GUARD = 1e-3
VMEM = pl.BlockSpec(memory_space=pltpu.VMEM)
SMEM = pl.BlockSpec(memory_space=pltpu.SMEM)


def call(body, outs, args, flops=10**6):
    in_specs = [SMEM if a.dtype == jnp.int32 else VMEM for a in args]
    shapes = [jax.ShapeDtypeStruct(s, F32) for s in outs]
    moved = 4 * sum(a.size for a in args)
    return pl.pallas_call(
        body,
        out_shape=shapes,
        in_specs=in_specs,
        out_specs=[VMEM] * len(shapes),
        compiler_params=pltpu.CompilerParams(vmem_limit_bytes=32 * 2**20),
        cost_estimate=pl.CostEstimate(flops=flops, bytes_accessed=moved, transcendentals=0),
    )(*args)


def lanes():
    return lax.broadcasted_iota(jnp.int32, TILE, 1)


def sublanes():
    return lax.broadcasted_iota(jnp.int32, TILE, 0)


def roll_lanes(x, shift):
    return pltpu.roll(x, shift % 128, 1)


def swap_groups(tiles):
    low = lanes() < 64
    even = (lanes() // 32) % 2 == 0
    a = [None] * 4
    for i in (0, 1):
        a[i] = jnp.where(low, tiles[i], roll_lanes(tiles[i + 2], 64))
        a[i + 2] = jnp.where(low, roll_lanes(tiles[i], 64), tiles[i + 2])
    out = []
    for i in (0, 2):
        out.append(jnp.where(even, a[i], roll_lanes(a[i + 1], 32)))
        out.append(jnp.where(even, roll_lanes(a[i], -32), a[i + 1]))
    return out


def owner(info, row):
    return jnp.where(info[4] == 1, ROW_OWNER[1][row], ROW_OWNER[0][row])


def pack_body(info, sources, links, out):
    for ref, base, chunks in ((sources, 0, 6), (links, 48, 9)):
        for z in range(2):
            for i in range(chunks):
                tiles = [ref[s, pl.ds(16 * i + z, 8, stride=2), :] for s in range(4)]
                for row, tile in enumerate(swap_groups(tiles)):
                    out[owner(info, row), z, base + 8 * i : base + 8 * i + 8, :] = tile


def unpack_body(info, received, links, spinor, *faces):
    for c in range(24):
        for t in range(2):
            spinor[c, t] = received[pl.ds(2 * c + t, 8, stride=120), :]
    low = lanes() < 64
    even = (lanes() // 32) % 2 == 0
    for l in range(36):
        for t in range(2):
            x = received[pl.ds(48 + 2 * l + t, 8, stride=120), :]
            half = roll_lanes(x, 64)
            for q, pair in ((0, jnp.where(low, x, half)), (2, jnp.where(low, half, x))):
                turned = roll_lanes(pair, 32)
                links[q * 36 + l, t] = jnp.where(even, pair, turned)
                links[(q + 1) * 36 + l, t] = jnp.where(even, turned, pair)
    write_faces(info, spinor, links, 1, faces)


def load_spinor(ref, t):
    return [[[ref[(p * 4 + s) * 3 + c, t] for c in range(3)] for s in range(4)] for p in range(2)]


def signed_add(a, b, sign):
    return a + b if sign > 0 else a - b


def turn(phase, part):
    if phase[1] == 0:
        return part, phase[0]
    return 1 - part, -phase[1] if part == 0 else phase[1]


def project(v, direction, hop):
    out = [[None, None], [None, None]]
    for part in range(2):
        for k in range(2):
            partner = GAMMA_COLUMNS[direction][k]
            other, sign = turn(GAMMA_PHASES[direction][k], part)
            out[part][k] = [
                signed_add(v[part][k][c], v[other][partner][c], sign * hop) for c in range(3)
            ]
    return out


def rebuild_add(acc, half, direction, hop):
    for part in range(2):
        for s in range(4):
            if s < 2:
                source, sign = half[part][s], 1
            else:
                other, sign = turn(GAMMA_PHASES[direction][s], part)
                source, sign = half[other][GAMMA_COLUMNS[direction][s]], sign * hop
            for c in range(3):
                old = acc[part][s][c]
                if old is None:
                    acc[part][s][c] = source[c] if sign > 0 else -source[c]
                else:
                    acc[part][s][c] = signed_add(old, source[c], sign)


def color_times(links, parity, direction, t, half, adjoint):
    base = (parity * 4 + direction) * 18
    out = [[[None] * 3 for _ in range(2)] for _ in range(2)]
    for row in range(3):
        for column in range(3):
            entry = 3 * column + row if adjoint else 3 * row + column
            re, im = links[base + entry, t], links[base + 9 + entry, t]
            for k in range(2):
                x, y = half[0][k][column], half[1][k][column]
                if adjoint:
                    a, b = re * x + im * y, re * y - im * x
                else:
                    a, b = re * x - im * y, re * y + im * x
                if out[0][k][row] is None:
                    out[0][k][row], out[1][k][row] = a, b
                else:
                    out[0][k][row] += a
                    out[1][k][row] += b
    return out


def map_half(f, half):
    return [[[f(x) for x in row] for row in part] for part in half]


def halves(half):
    return [half[p][k][c] for p in range(2) for k in range(2) for c in range(3)]


def write_faces(info, spinor, links, parity, faces):
    time_a, time_b, row_a, row_b = faces
    time_odd, row_odd = info[0] == 1, info[1] == 1
    for t in range(2):
        v = load_spinor(spinor, t)
        down = halves(project(v, 1, -1))
        up = halves(color_times(links, 1 - parity, 1, t, project(v, 1, 1), True))
        for i in range(12):
            row_a[i, t] = jnp.where(row_odd, down[i], up[i])
            row_b[i, t] = jnp.where(row_odd, up[i], down[i])
        if t == 0:
            time_down = halves(project(v, 3, -1))
        else:
            time_up = halves(color_times(links, 1 - parity, 3, t, project(v, 3, 1), True))
    for i in range(12):
        time_a[i] = jnp.where(time_odd, time_down[i], time_up[i])
        time_b[i] = jnp.where(time_odd, time_up[i], time_down[i])


def inner_body(parity, with_moments, info, spinor, links, out, *moments):
    cell = lanes() % 32
    site = sublanes() + info[1] + parity
    vs = [load_spinor(spinor, t) for t in range(2)]
    for t in range(2):
        odd = (site + t) % 2 == 1
        v = vs[t]
        acc = [[[None] * 3 for _ in range(4)] for _ in range(2)]

        def next_cell(x):
            moved = jnp.where(cell == 31, roll_lanes(x, 31), roll_lanes(x, -1))
            return jnp.where(odd, moved, x)

        def prior_cell(x):
            moved = jnp.where(cell == 0, roll_lanes(x, -31), roll_lanes(x, 1))
            return jnp.where(odd, x, moved)

        half = map_half(next_cell, project(v, 0, -1))
        rebuild_add(acc, color_times(links, parity, 0, t, half, False), 0, -1)
        half = color_times(links, 1 - parity, 0, t, project(v, 0, 1), True)
        rebuild_add(acc, map_half(prior_cell, half), 0, 1)
        half = map_half(lambda x: pltpu.roll(x, 7, 0), project(v, 2, -1))
        rebuild_add(acc, color_times(links, parity, 2, t, half, False), 2, -1)
        half = color_times(links, 1 - parity, 2, t, project(v, 2, 1), True)
        rebuild_add(acc, map_half(lambda x: pltpu.roll(x, 1, 0), half), 2, 1)
        if t == 0:
            half = project(vs[1], 3, -1)
            rebuild_add(acc, color_times(links, parity, 3, 0, half, False), 3, -1)
        else:
            half = color_times(links, 1 - parity, 3, 0, project(vs[0], 3, 1), True)
            rebuild_add(acc, half, 3, 1)
        for p in range(2):
            for s in range(4):
                for c in range(3):
                    out[(p * 4 + s) * 3 + c, t] = acc[p][s][c]
    if with_moments:
        for i, total in enumerate(moment_tiles(spinor)):
            moments[0][i] = total


def moment_tiles(spinor):
    totals = [jnp.zeros(TILE, F32) for _ in range(5)]
    for t in range(2):
        for c in range(12):
            re, im = spinor[c, t], spinor[12 + c, t]
            totals[0] = totals[0] + (re * re + im * im)
            for d in (1, 2):
                re_d, im_d = roll_lanes(re, -32 * d), roll_lanes(im, -32 * d)
                totals[2 * d - 1] = totals[2 * d - 1] + (re * re_d + im * im_d)
                totals[2 * d] = totals[2 * d] + (re * im_d - im * re_d)
    return totals


def add_received(info, acc, links, parity, t, recv):
    time_a, time_b, row_a, row_b = recv
    time_odd, row_odd = info[0] == 1, info[1] == 1

    def pick(flag, first, second):
        flat = [jnp.where(flag, first[i], second[i]) for i in range(12)]
        return [[flat[6 * p + 3 * k : 6 * p + 3 * k + 3] for k in range(2)] for p in range(2)]

    half = pick(row_odd, [row_b[i, t] for i in range(12)], [row_a[i, t] for i in range(12)])
    rebuild_add(acc, color_times(links, parity, 1, t, half, False), 1, -1)
    half = pick(row_odd, [row_a[i, t] for i in range(12)], [row_b[i, t] for i in range(12)])
    rebuild_add(acc, half, 1, 1)
    a, b = [time_a[i] for i in range(12)], [time_b[i] for i in range(12)]
    if t == 1:
        sign = jnp.where(info[2] == 1, -1.0, 1.0)
        half = map_half(lambda x: x * sign, pick(time_odd, b, a))
        rebuild_add(acc, color_times(links, parity, 3, t, half, False), 3, -1)
    else:
        sign = jnp.where(info[3] == 1, -1.0, 1.0)
        half = map_half(lambda x: x * sign, pick(time_odd, a, b))
        rebuild_add(acc, half, 3, 1)


def finished_spinor(info, partial, links, parity, t, recv, base):
    acc = load_spinor(partial, t)
    add_received(info, acc, links, parity, t, recv)
    if base is None:
        return acc
    old = load_spinor(base, t)
    for p in range(2):
        for s in range(4):
            for c in range(3):
                hopped = KAPPA_SQUARE * acc[p][s][c]
                acc[p][s][c] = old[p][s][c] - hopped if s < 2 else hopped - old[p][s][c]
    return acc


def outer_body(parity, with_base, with_faces, *refs):
    info, partial, links = refs[:3]
    recv = refs[3:7]
    base = refs[7] if with_base else None
    out = refs[8] if with_base else refs[7]
    faces = refs[-4:]
    for t in range(2):
        acc = finished_spinor(info, partial, links, parity, t, recv, base)
        for p in range(2):
            for s in range(4):
                for c in range(3):
                    out[(p * 4 + s) * 3 + c, t] = acc[p][s][c]
    if with_faces:
        write_faces(info, out, links, 1 - parity, faces)


def group_sum(x):
    cell = lax.broadcasted_iota(jnp.int32, x.shape, 1) % 32
    for step in (16, 8, 4, 2, 1):
        x = x + jnp.where(cell < 32 - step, roll_lanes(x, -step), roll_lanes(x, 32 - step))
    return x


def pick_cells(scratch, out):
    rows = group_sum(scratch[...])
    cell = lax.broadcasted_iota(jnp.int32, rows.shape, 1) % 32
    line = lax.broadcasted_iota(jnp.int32, rows.shape, 0)
    packed = jnp.sum(jnp.where(cell == line, rows, 0.0), axis=0, keepdims=True)
    out[...] = jnp.broadcast_to(packed, out.shape)


def moments_body(spinor, *refs):
    given, out, scratch = refs[:-2], refs[-2], refs[-1]
    scratch[...] = jnp.zeros(scratch.shape, F32)
    at = 0
    for total in [[m[i] for i in range(5)] for m in given] + [moment_tiles(spinor)]:
        for tile in total:
            scratch[at : at + 1, :] = jnp.sum(tile, axis=0, keepdims=True)
            at += 1
    pick_cells(scratch, out)


def moments_call(spinor, given):
    args = (spinor, *given)
    return pl.pallas_call(
        moments_body,
        out_shape=jax.ShapeDtypeStruct((32, 128), F32),
        in_specs=[VMEM] * len(args),
        out_specs=VMEM,
        scratch_shapes=[pltpu.VMEM((24, 128), F32)],
        cost_estimate=pl.CostEstimate(flops=10**5, bytes_accessed=10**5, transcendentals=0),
    )(*args)


def row_sum_body(rows, out):
    out[...] = jnp.broadcast_to(jnp.sum(rows[...], axis=0, keepdims=True), out.shape)


def reduce_devices(rows):
    rows = lax.all_to_all(rows, ("gz", "gy"), 0, 0, tiled=True)
    (rows,) = call(row_sum_body, [(16, 128)], (rows,), 10**4)
    return lax.all_to_all(rows, "ta", 0, 0, tiled=True)


def group_of_lane():
    return lanes() // 32


def read_matrix(total, field):
    line, group = sublanes(), group_of_lane()
    re, im = jnp.zeros(TILE, F32), jnp.zeros(TILE, F32)

    def value(q, g):
        lane = 32 * g + 5 * field + q
        return jnp.broadcast_to(total[:, lane : lane + 1], TILE)

    for i in range(4):
        re = jnp.where((line == i) & (group == i), value(0, i), re)
        for d in (1, 2):
            if d == 2 and i >= 2:
                continue
            j = (i + d) % 4
            x, y = value(2 * d - 1, i), value(2 * d, i)
            here, there = (line == i) & (group == j), (line == j) & (group == i)
            re = jnp.where(here | there, x, re)
            im = jnp.where(here, y, jnp.where(there, -y, im))
    return re, im


def column(x, k):
    return jnp.broadcast_to(x[:, 32 * k : 32 * k + 1], TILE)


def line_of(x, k):
    return jnp.broadcast_to(x[k : k + 1, :], TILE)


def matmul(a, b):
    re, im = jnp.zeros(TILE, F32), jnp.zeros(TILE, F32)
    for k in range(4):
        ar, ai, br, bi = column(a[0], k), column(a[1], k), line_of(b[0], k), line_of(b[1], k)
        re = re + (ar * br - ai * bi)
        im = im + (ar * bi + ai * br)
    return re, im


def adjoint_matmul(a, b):
    line, group = sublanes(), group_of_lane()
    re, im = jnp.zeros(TILE, F32), jnp.zeros(TILE, F32)
    for k in range(4):
        ar, ai = jnp.zeros(TILE, F32), jnp.zeros(TILE, F32)
        for i in range(4):
            here = line == i
            ar = jnp.where(here, jnp.broadcast_to(a[0][k : k + 1, 32 * i : 32 * i + 1], TILE), ar)
            ai = jnp.where(here, jnp.broadcast_to(a[1][k : k + 1, 32 * i : 32 * i + 1], TILE), ai)
        br, bi = line_of(b[0], k), line_of(b[1], k)
        re = re + (ar * br + ai * bi)
        im = im + (ar * bi - ai * br)
    return re, im


def solve(c, e, lowest):
    line = sublanes()
    cr, ci, er, ei = c[0], c[1], e[0], e[1]
    good = None
    for k in range(4):
        pivot = jnp.broadcast_to(cr[k : k + 1, 32 * k : 32 * k + 1], TILE)
        floor = jnp.broadcast_to(lowest[k : k + 1, 32 * k : 32 * k + 1], TILE)
        here = pivot > floor
        good = here if good is None else good & here
        inverse = 1.0 / pivot
        rows = [line_of(x, k) * inverse for x in (cr, ci, er, ei)]
        fr, fi = column(cr, k), column(ci, k)
        at = line == k
        cr, ci = (
            jnp.where(at, rows[0], cr - (fr * rows[0] - fi * rows[1])),
            jnp.where(at, rows[1], ci - (fr * rows[1] + fi * rows[0])),
        )
        er, ei = (
            jnp.where(at, rows[2], er - (fr * rows[2] - fi * rows[3])),
            jnp.where(at, rows[3], ei - (fr * rows[3] + fi * rows[2])),
        )
    return (er, ei), good


def add(a, b):
    return a[0] + b[0], a[1] + b[1]


def sub(a, b):
    return a[0] - b[0], a[1] - b[1]


def write_coefficients(out, base, c):
    line, group = sublanes(), group_of_lane()
    for d in range(4):
        here = line == (group + d) % 4
        for part in range(2):
            row = jnp.sum(jnp.where(here, c[part], 0.0), axis=0, keepdims=True)
            out[base + 2 * d + part : base + 2 * d + part + 1, :] = row


def coefficients_body(rows, out, good_out):
    total = jnp.sum(rows[...], axis=0, keepdims=True)
    mu = [read_matrix(total, f) for f in range(4)]
    line, group = sublanes(), group_of_lane()
    diagonal = (line == group) & (line < 4)
    unit = jnp.where(diagonal, 1.0, 0.0)
    alpha, good1 = solve(mu[1], mu[0], PIVOT_GUARD * mu[1][0])
    quad = adjoint_matmul(alpha, matmul(mu[2], alpha))
    right = matmul(mu[1], alpha)
    left = adjoint_matmul(alpha, mu[1])
    rho = add(sub(quad, add(left, right)), mu[0])
    rho_size = jnp.abs(quad[0]) + jnp.abs(left[0]) + jnp.abs(right[0]) + jnp.abs(mu[0][0])
    beta, good0 = solve(mu[0], rho, PIVOT_GUARD * mu[0][0])
    p = (beta[0] + unit, beta[1])
    first = adjoint_matmul(p, matmul(mu[1], p))
    cross = adjoint_matmul(p, matmul(mu[2], alpha))
    cross2 = adjoint_matmul(alpha, matmul(mu[2], p))
    last = adjoint_matmul(alpha, matmul(mu[3], alpha))
    c = add(sub(first, add(cross, cross2)), last)
    c_size = jnp.abs(first[0]) + jnp.abs(cross[0]) + jnp.abs(cross2[0]) + jnp.abs(last[0])
    alpha1, good2 = solve(c, rho, GUARD * c_size)
    _, good3 = solve(rho, unit_pair(unit), GUARD * rho_size)
    q = matmul(alpha, alpha1)
    k = add(alpha, matmul(p, alpha1))
    write_coefficients(out, 0, k)
    write_coefficients(out, 8, q)
    good = good0 & good1 & good2 & good3
    good_out[...] = jnp.where(good, 1.0, 0.0)


def unit_pair(unit):
    return unit, jnp.zeros(TILE, F32)


def solve_body(which, c_rows, e_rows, out):
    c = read_matrix(jnp.sum(c_rows[...], axis=0, keepdims=True), which[0])
    e = read_matrix(jnp.sum(e_rows[...], axis=0, keepdims=True), which[1])
    solved, _ = solve(c, e, jnp.zeros(TILE, F32))
    write_coefficients(out, 0, solved)


def mix(re, im, coefficients, base):
    total_re = total_im = None
    for d in range(4):
        x, y = (re, im) if d == 0 else (roll_lanes(re, -32 * d), roll_lanes(im, -32 * d))
        cr = coefficients[base + 2 * d : base + 2 * d + 1, :]
        ci = coefficients[base + 2 * d + 1 : base + 2 * d + 2, :]
        a, b = x * cr - y * ci, x * ci + y * cr
        total_re = a if total_re is None else total_re + a
        total_im = b if total_im is None else total_im + b
    return total_re, total_im


def combine_body(sign, x, y, coefficients, out):
    for t in range(2):
        for c in range(12):
            re, im = mix(y[c, t], y[12 + c, t], coefficients, 0)
            out[c, t] = signed_add(x[c, t], re, sign)
            out[12 + c, t] = signed_add(x[12 + c, t], im, sign)


def final_body(info, partial, links, time_a, time_b, row_a, row_b, base, first, image, rows, out):
    recv = (time_a, time_b, row_a, row_b)
    for t in range(2):
        b = finished_spinor(info, partial, links, 0, t, recv, base)
        for s in range(4):
            for c in range(3):
                at = s * 3 + c
                re, im = first[at, t], first[12 + at, t]
                image_re, image_im = image[at, t], image[12 + at, t]
                rk = mix(re, im, rows, 0)
                ak = mix(image_re, image_im, rows, 0)
                aq = mix(image_re, image_im, rows, 8)
                bq = mix(b[0][s][c], b[1][s][c], rows, 8)
                out[pl.ds(2 * at + t, 8, stride=96), :] = rk[0] - aq[0]
                out[pl.ds(2 * (12 + at) + t, 8, stride=96), :] = rk[1] - aq[1]
                out[pl.ds(48 + 2 * at + t, 8, stride=96), :] = re - ak[0] + bq[0]
                out[pl.ds(48 + 2 * (12 + at) + t, 8, stride=96), :] = im - ak[1] + bq[1]


def send_order_body(solution_ref, residual_ref, out):
    for i, ref in enumerate((solution_ref, residual_ref)):
        for c in range(24):
            for t in range(2):
                out[pl.ds(48 * i + 2 * c + t, 8, stride=96), :] = ref[c, t]


def deliver_body(info, received, solution_ref, residual_ref):
    for i, ref in enumerate((solution_ref, residual_ref)):
        for z in range(2):
            for n in range(6):
                at = 48 * i + 8 * n
                tiles = [received[owner(info, row), z, at : at + 8, :] for row in range(4)]
                for s, tile in enumerate(swap_groups(tiles)):
                    ref[s, pl.ds(16 * n + z, 8, stride=2), :] = tile


SPINOR = (24, 2, 8, 128)
FACES = [(12, 8, 128), (12, 8, 128), (12, 2, 8, 128), (12, 2, 8, 128)]


def make_pairs(order, start):
    count = len(order)
    out = []
    for i in range(start, start + count, 2):
        a, b = order[i % count], order[(i + 1) % count]
        out += [(a, b), (b, a)]
    return out


def exchange(faces):
    times = list(range(lax.axis_size("ta")))
    blocks = lax.axis_size("gy")
    rows = [gz * blocks + gy for gy in range(blocks) for gz in ROW_OWNER[gy % 2]]
    time_a, time_b, row_a, row_b = faces
    return (
        lax.ppermute(time_a, "ta", make_pairs(times, 0)),
        lax.ppermute(time_b, "ta", make_pairs(times, 1)),
        lax.ppermute(row_a, ("gz", "gy"), make_pairs(rows, 0)),
        lax.ppermute(row_b, ("gz", "gy"), make_pairs(rows, 1)),
    )


def hop_inner(info, spinor, links, parity, with_moments=False):
    outs = [SPINOR] + ([(5, 8, 128)] if with_moments else [])

    def body(*refs):
        inner_body(parity, with_moments, *refs)

    return call(body, outs, (info, spinor, links), 8 * 10**6)


def hop_outer(info, partial, links, recv, parity, base=None, with_faces=True):
    args = (info, partial, links, *recv) + (() if base is None else (base,))

    def body(*refs):
        outer_body(parity, base is not None, with_faces, *refs)

    outs = call(body, [SPINOR] + (FACES if with_faces else []), args, 4 * 10**6)
    return outs[0], outs[1:]


def half_normal(info, spinor, faces, links, with_moments=False, with_faces=True):
    recv = exchange(faces)
    partial, *moments = hop_inner(info, spinor, links, 1, with_moments)
    odd, faces = hop_outer(info, partial, links, recv, 1)
    recv = exchange(faces)
    (partial,) = hop_inner(info, odd, links, 0)
    out, faces = hop_outer(info, partial, links, recv, 0, spinor, with_faces)
    return out, faces, moments


def faces_only(info, spinor, links):
    def body(info, spinor, links, *faces):
        write_faces(info, spinor, links, 1, faces)

    return call(body, FACES, (info, spinor, links))


def direct_branch(info, links, first, image, rows):
    def solve_call(c_rows, e_rows, c_field, e_field):
        def body(*refs):
            solve_body((c_field, e_field), *refs)

        return call(body, [(8, 128)], (c_rows, e_rows), 10**4)[0]

    def combine(sign, x, y, coefficients):
        def body(*refs):
            combine_body(sign, *refs)

        return call(body, [SPINOR], (x, y, coefficients))[0]

    alpha = solve_call(rows, rows, 1, 0)
    residual = combine(-1, first, image, alpha)
    rho = reduce_devices(moments_call(residual, ()))
    beta = solve_call(rows, rho, 0, 0)
    search = combine(1, residual, first, beta)
    faces = faces_only(info, search, links)
    halfway, faces, _ = half_normal(info, search, faces, links)
    curvature = reduce_devices(moments_call(halfway, ()))
    images, _, _ = half_normal(info, halfway, faces, links, with_faces=False)
    alpha1 = solve_call(curvature, rho, 0, 0)
    zero = jnp.zeros(SPINOR, F32)
    solution_field = combine(1, combine(1, zero, first, alpha), search, alpha1)
    residual = combine(-1, residual, images, alpha1)
    return call(send_order_body, [(768, 128)], (solution_field, residual))[0]


def local(sources, gauge_links):
    ta, gz, gy = (lax.axis_index(name) for name in ("ta", "gz", "gy"))
    odd_block = gy % 2
    position = jnp.where(odd_block == 1, jnp.array([3, 2, 0, 1])[gz], jnp.array([0, 1, 3, 2])[gz])
    info = jnp.stack(
        [ta % 2, position % 2, ta == lax.axis_size("ta") - 1, ta == 0, odd_block]
    ).astype(jnp.int32)

    args = (info, sources.reshape(4, 96, 128), gauge_links.reshape(4, 144, 128))
    (packed,) = call(pack_body, [(4, 2, 120, 128)], args)
    received = lax.all_to_all(packed, "gz", 0, 0).reshape(960, 128)
    links, first, *faces = call(
        unpack_body, [(144, 2, 8, 128), SPINOR] + FACES, (info, received)
    )
    half1, faces, moments0 = half_normal(info, first, faces, links, True)
    image, faces, moments1 = half_normal(info, half1, faces, links, True)
    half2, faces, moments2 = half_normal(info, image, faces, links, True)
    rows = reduce_devices(moments_call(half2, (*moments0, *moments1, *moments2)))
    table, good = call(coefficients_body, [(16, 128), TILE], (rows,), 10**5)

    recv = exchange(faces)
    (partial,) = hop_inner(info, half2, links, 1)
    odd, faces = hop_outer(info, partial, links, recv, 1)
    recv = exchange(faces)
    (partial,) = hop_inner(info, odd, links, 0)

    def moment_branch():
        given = (info, partial, links, *recv, half2, first, image, table)
        return call(final_body, [(768, 128)], given, 10**7)[0]

    out = lax.cond(
        good[0, 0] > 0.5,
        moment_branch,
        lambda: direct_branch(info, links, first, image, rows),
    )
    received = lax.all_to_all(out.reshape(4, 2, 96, 128), "gz", 0, 0)
    done = call(deliver_body, [(4, 96, 128)] * 2, (info, received))
    return tuple(x.reshape(sources.shape) for x in done)


def solution(mesh):
    spinor_spec = P(None, None, None, None, "ta", "gz", "gy")
    link_spec = P(None, None, None, None, None, "ta", "gz", "gy")
    return jax.shard_map(
        local,
        mesh=mesh,
        in_specs=(spinor_spec, link_spec),
        out_specs=(spinor_spec, spinor_spec),
        check_vma=False,
    )
```

```python
import jax
import jax.numpy as jnp
from jax import lax
from jax.experimental import pallas as pl
from jax.experimental.pallas import tpu as pltpu
from jax.sharding import PartitionSpec as P

SRC = 4
KAPPA_SQUARE = 0.0196
GAMMA_COLUMNS = ((3, 2, 1, 0), (3, 2, 1, 0), (2, 3, 0, 1), (2, 3, 0, 1))
GAMMA_PHASES = (
    ((0, 1), (0, 1), (0, -1), (0, -1)),
    ((1, 0), (-1, 0), (-1, 0), (1, 0)),
    ((0, 1), (0, -1), (0, -1), (0, 1)),
    ((1, 0), (1, 0), (1, 0), (1, 0)),
)
F32 = jnp.float32
TILE = (8, 128)
ROW_OWNER = ((0, 1, 3, 2), (2, 3, 1, 0))
GUARD = 0.005
PIVOT_GUARD = 1e-3
VMEM = pl.BlockSpec(memory_space=pltpu.VMEM)
SMEM = pl.BlockSpec(memory_space=pltpu.SMEM)
ANY = pl.BlockSpec(memory_space=pl.ANY)


def call(body, outs, args, flops=10**6, after=(), scratch=(), flag=False):
    count = len(args)

    def without_after(*refs):
        body(*refs[:count], *refs[count + len(after) :])

    shapes = [jax.ShapeDtypeStruct(s, F32) for s in outs]
    out_specs = [VMEM] * len(shapes)
    if flag:
        shapes.append(jax.ShapeDtypeStruct((1,), jnp.int32))
        out_specs.append(SMEM)
    moved = 4 * sum(a.size for a in args)
    return pl.pallas_call(
        without_after,
        out_shape=shapes,
        in_specs=[VMEM] * count + [ANY] * len(after),
        out_specs=out_specs,
        scratch_shapes=scratch,
        compiler_params=pltpu.CompilerParams(vmem_limit_bytes=16 * 2**20),
        cost_estimate=pl.CostEstimate(flops=flops, bytes_accessed=moved, transcendentals=0),
    )(*args, *after)


def place():
    ta, gz, gy = (lax.axis_index(name) for name in ("ta", "gz", "gy"))
    block_odd = gy % 2
    row_odd = (gz + gz // 2 + block_odd) % 2
    return ta % 2, row_odd, ta == lax.axis_size("ta") - 1, ta == 0, block_odd


def lanes():
    return lax.broadcasted_iota(jnp.int32, TILE, 1)


def sublanes():
    return lax.broadcasted_iota(jnp.int32, TILE, 0)


def roll_lanes(x, shift):
    return pltpu.roll(x, shift % 128, 1)


def swap_groups(tiles):
    low = lanes() < 64
    even = (lanes() // 32) % 2 == 0
    a = [None] * 4
    for i in (0, 1):
        a[i] = jnp.where(low, tiles[i], roll_lanes(tiles[i + 2], 64))
        a[i + 2] = jnp.where(low, roll_lanes(tiles[i], 64), tiles[i + 2])
    out = []
    for i in (0, 2):
        out.append(jnp.where(even, a[i], roll_lanes(a[i + 1], 32)))
        out.append(jnp.where(even, roll_lanes(a[i], -32), a[i + 1]))
    return out


def owner(block_odd, row):
    return jnp.where(block_odd == 1, ROW_OWNER[1][row], ROW_OWNER[0][row])


def pack_body(sources, links, out):
    block_odd = place()[4]
    for ref, base, chunks in ((sources, 0, 6), (links, 48, 9)):
        for z in range(2):
            for i in range(chunks):
                tiles = [ref[s, pl.ds(16 * i + z, 8, stride=2), :] for s in range(4)]
                for row, tile in enumerate(swap_groups(tiles)):
                    out[owner(block_odd, row), z, base + 8 * i : base + 8 * i + 8, :] = tile


def unpack_body(received, links, spinor, *faces):
    for c in range(24):
        for t in range(2):
            spinor[c, t] = received[pl.ds(2 * c + t, 8, stride=120), :]
    low = lanes() < 64
    even = (lanes() // 32) % 2 == 0
    for l in range(36):
        for t in range(2):
            x = received[pl.ds(48 + 2 * l + t, 8, stride=120), :]
            half = roll_lanes(x, 64)
            for q, pair in ((0, jnp.where(low, x, half)), (2, jnp.where(low, half, x))):
                turned = roll_lanes(pair, 32)
                links[q * 36 + l, t] = jnp.where(even, pair, turned)
                links[(q + 1) * 36 + l, t] = jnp.where(even, turned, pair)
    write_faces(spinor, links, 1, faces)


def load_spinor(ref, t):
    return [[[ref[(p * 4 + s) * 3 + c, t] for c in range(3)] for s in range(4)] for p in range(2)]


def signed_add(a, b, sign):
    return a + b if sign > 0 else a - b


def turn(phase, part):
    if phase[1] == 0:
        return part, phase[0]
    return 1 - part, -phase[1] if part == 0 else phase[1]


def project(v, direction, hop):
    out = [[None, None], [None, None]]
    for part in range(2):
        for k in range(2):
            partner = GAMMA_COLUMNS[direction][k]
            other, sign = turn(GAMMA_PHASES[direction][k], part)
            out[part][k] = [
                signed_add(v[part][k][c], v[other][partner][c], sign * hop) for c in range(3)
            ]
    return out


def rebuild_add(acc, half, direction, hop):
    for part in range(2):
        for s in range(4):
            if s < 2:
                source, sign = half[part][s], 1
            else:
                other, sign = turn(GAMMA_PHASES[direction][s], part)
                source, sign = half[other][GAMMA_COLUMNS[direction][s]], sign * hop
            for c in range(3):
                old = acc[part][s][c]
                if old is None:
                    acc[part][s][c] = source[c] if sign > 0 else -source[c]
                else:
                    acc[part][s][c] = signed_add(old, source[c], sign)


def color_times(links, parity, direction, t, half, adjoint):
    base = (parity * 4 + direction) * 18
    out = [[[None] * 3 for _ in range(2)] for _ in range(2)]
    for row in range(3):
        for column in range(3):
            entry = 3 * column + row if adjoint else 3 * row + column
            re, im = links[base + entry, t], links[base + 9 + entry, t]
            for k in range(2):
                x, y = half[0][k][column], half[1][k][column]
                if adjoint:
                    a, b = re * x + im * y, re * y - im * x
                else:
                    a, b = re * x - im * y, re * y + im * x
                if out[0][k][row] is None:
                    out[0][k][row], out[1][k][row] = a, b
                else:
                    out[0][k][row] += a
                    out[1][k][row] += b
    return out


def map_half(f, half):
    return [[[f(x) for x in row] for row in part] for part in half]


def halves(half):
    return [half[p][k][c] for p in range(2) for k in range(2) for c in range(3)]


def write_faces(spinor, links, parity, faces):
    time_a, time_b, row_a, row_b = faces
    time_odd, row_odd = (flag == 1 for flag in place()[:2])
    for t in range(2):
        v = load_spinor(spinor, t)
        down = halves(project(v, 1, -1))
        up = halves(color_times(links, 1 - parity, 1, t, project(v, 1, 1), True))
        for i in range(12):
            row_a[i, t] = jnp.where(row_odd, down[i], up[i])
            row_b[i, t] = jnp.where(row_odd, up[i], down[i])
        if t == 0:
            time_down = halves(project(v, 3, -1))
        else:
            time_up = halves(color_times(links, 1 - parity, 3, t, project(v, 3, 1), True))
    for i in range(12):
        time_a[i] = jnp.where(time_odd, time_down[i], time_up[i])
        time_b[i] = jnp.where(time_odd, time_up[i], time_down[i])


def inner_body(parity, with_moments, spinor, links, out, *moments):
    cell = lanes() % 32
    site = sublanes() + place()[1] + parity
    vs = [load_spinor(spinor, t) for t in range(2)]
    for t in range(2):
        odd = (site + t) % 2 == 1
        v = vs[t]
        acc = [[[None] * 3 for _ in range(4)] for _ in range(2)]

        def next_cell(x):
            moved = jnp.where(cell == 31, roll_lanes(x, 31), roll_lanes(x, -1))
            return jnp.where(odd, moved, x)

        def prior_cell(x):
            moved = jnp.where(cell == 0, roll_lanes(x, -31), roll_lanes(x, 1))
            return jnp.where(odd, x, moved)

        half = map_half(next_cell, project(v, 0, -1))
        rebuild_add(acc, color_times(links, parity, 0, t, half, False), 0, -1)
        half = color_times(links, 1 - parity, 0, t, project(v, 0, 1), True)
        rebuild_add(acc, map_half(prior_cell, half), 0, 1)
        half = map_half(lambda x: pltpu.roll(x, 7, 0), project(v, 2, -1))
        rebuild_add(acc, color_times(links, parity, 2, t, half, False), 2, -1)
        half = color_times(links, 1 - parity, 2, t, project(v, 2, 1), True)
        rebuild_add(acc, map_half(lambda x: pltpu.roll(x, 1, 0), half), 2, 1)
        if t == 0:
            half = project(vs[1], 3, -1)
            rebuild_add(acc, color_times(links, parity, 3, 0, half, False), 3, -1)
        else:
            half = color_times(links, 1 - parity, 3, 0, project(vs[0], 3, 1), True)
            rebuild_add(acc, half, 3, 1)
        for p in range(2):
            for s in range(4):
                for c in range(3):
                    out[(p * 4 + s) * 3 + c, t] = acc[p][s][c]
    if with_moments:
        for i, total in enumerate(moment_tiles(spinor)):
            moments[0][i] = total


def moment_tiles(spinor):
    totals = [jnp.zeros(TILE, F32) for _ in range(5)]
    for t in range(2):
        for c in range(12):
            re, im = spinor[c, t], spinor[12 + c, t]
            totals[0] = totals[0] + (re * re + im * im)
            for d in (1, 2):
                re_d, im_d = roll_lanes(re, -32 * d), roll_lanes(im, -32 * d)
                totals[2 * d - 1] = totals[2 * d - 1] + (re * re_d + im * im_d)
                totals[2 * d] = totals[2 * d] + (re * im_d - im * re_d)
    return totals


def add_received(acc, links, parity, t, recv):
    time_a, time_b, row_a, row_b = recv
    time_odd, row_odd, last, first, _ = place()
    time_odd, row_odd = time_odd == 1, row_odd == 1

    def pick(flag, first, second):
        flat = [jnp.where(flag, first[i], second[i]) for i in range(12)]
        return [[flat[6 * p + 3 * k : 6 * p + 3 * k + 3] for k in range(2)] for p in range(2)]

    half = pick(row_odd, [row_b[i, t] for i in range(12)], [row_a[i, t] for i in range(12)])
    rebuild_add(acc, color_times(links, parity, 1, t, half, False), 1, -1)
    half = pick(row_odd, [row_a[i, t] for i in range(12)], [row_b[i, t] for i in range(12)])
    rebuild_add(acc, half, 1, 1)
    a, b = [time_a[i] for i in range(12)], [time_b[i] for i in range(12)]
    if t == 1:
        sign = jnp.where(last, -1.0, 1.0)
        half = map_half(lambda x: x * sign, pick(time_odd, b, a))
        rebuild_add(acc, color_times(links, parity, 3, t, half, False), 3, -1)
    else:
        sign = jnp.where(first, -1.0, 1.0)
        half = map_half(lambda x: x * sign, pick(time_odd, a, b))
        rebuild_add(acc, half, 3, 1)


def finished_spinor(partial, links, parity, t, recv, base):
    acc = load_spinor(partial, t)
    add_received(acc, links, parity, t, recv)
    if base is None:
        return acc
    old = load_spinor(base, t)
    for p in range(2):
        for s in range(4):
            for c in range(3):
                hopped = KAPPA_SQUARE * acc[p][s][c]
                acc[p][s][c] = old[p][s][c] - hopped if s < 2 else hopped - old[p][s][c]
    return acc


def outer_body(parity, with_base, with_faces, *refs):
    partial, links = refs[:2]
    recv = in_face_order(refs[2:6])
    base = refs[6] if with_base else None
    out = refs[7] if with_base else refs[6]
    faces = refs[-4:]
    for t in range(2):
        acc = finished_spinor(partial, links, parity, t, recv, base)
        for p in range(2):
            for s in range(4):
                for c in range(3):
                    out[(p * 4 + s) * 3 + c, t] = acc[p][s][c]
    if with_faces:
        write_faces(out, links, 1 - parity, faces)


def group_sum(x):
    cell = lax.broadcasted_iota(jnp.int32, x.shape, 1) % 32
    for step in (16, 8, 4, 2, 1):
        x = x + jnp.where(cell < 32 - step, roll_lanes(x, -step), roll_lanes(x, 32 - step))
    return x


def pick_cells(scratch, out):
    rows = group_sum(scratch[...])
    cell = lax.broadcasted_iota(jnp.int32, rows.shape, 1) % 32
    line = lax.broadcasted_iota(jnp.int32, rows.shape, 0)
    packed = jnp.sum(jnp.where(cell == line, rows, 0.0), axis=0, keepdims=True)
    out[...] = jnp.broadcast_to(packed, out.shape)


def moments_body(spinor, *refs):
    given, out, scratch = refs[:-2], refs[-2], refs[-1]
    scratch[...] = jnp.zeros(scratch.shape, F32)
    at = 0
    for total in [[m[i] for i in range(5)] for m in given] + [moment_tiles(spinor)]:
        for tile in total:
            scratch[at : at + 1, :] = jnp.sum(tile, axis=0, keepdims=True)
            at += 1
    pick_cells(scratch, out)


def moments_call(spinor, given):
    scratch = [pltpu.VMEM((24, 128), F32)]
    return call(moments_body, [(32, 128)], (spinor, *given), 10**5, scratch=scratch)[0]


def row_sum_body(rows, out):
    out[...] = jnp.broadcast_to(jnp.sum(rows[...], axis=0, keepdims=True), out.shape)


def reduce_rows(rows):
    rows = lax.all_to_all(rows, ("gz", "gy"), 0, 0, tiled=True)
    return call(row_sum_body, [(16, 128)], (rows,), 10**4)[0]


def reduce_devices(rows):
    return lax.all_to_all(reduce_rows(rows), "ta", 0, 0, tiled=True)


def group_of_lane():
    return lanes() // 32


def read_matrix(total, field):
    line, group = sublanes(), group_of_lane()
    re, im = jnp.zeros(TILE, F32), jnp.zeros(TILE, F32)

    def value(q, g):
        lane = 32 * g + 5 * field + q
        return jnp.broadcast_to(total[:, lane : lane + 1], TILE)

    for i in range(4):
        re = jnp.where((line == i) & (group == i), value(0, i), re)
        for d in (1, 2):
            if d == 2 and i >= 2:
                continue
            j = (i + d) % 4
            x, y = value(2 * d - 1, i), value(2 * d, i)
            here, there = (line == i) & (group == j), (line == j) & (group == i)
            re = jnp.where(here | there, x, re)
            im = jnp.where(here, y, jnp.where(there, -y, im))
    return re, im


def column(x, k):
    return jnp.broadcast_to(x[:, 32 * k : 32 * k + 1], TILE)


def line_of(x, k):
    return jnp.broadcast_to(x[k : k + 1, :], TILE)


def matmul(a, b):
    re, im = jnp.zeros(TILE, F32), jnp.zeros(TILE, F32)
    for k in range(4):
        ar, ai, br, bi = column(a[0], k), column(a[1], k), line_of(b[0], k), line_of(b[1], k)
        re = re + (ar * br - ai * bi)
        im = im + (ar * bi + ai * br)
    return re, im


def adjoint_matmul(a, b):
    line, group = sublanes(), group_of_lane()
    re, im = jnp.zeros(TILE, F32), jnp.zeros(TILE, F32)
    for k in range(4):
        ar, ai = jnp.zeros(TILE, F32), jnp.zeros(TILE, F32)
        for i in range(4):
            here = line == i
            ar = jnp.where(here, jnp.broadcast_to(a[0][k : k + 1, 32 * i : 32 * i + 1], TILE), ar)
            ai = jnp.where(here, jnp.broadcast_to(a[1][k : k + 1, 32 * i : 32 * i + 1], TILE), ai)
        br, bi = line_of(b[0], k), line_of(b[1], k)
        re = re + (ar * br + ai * bi)
        im = im + (ar * bi - ai * br)
    return re, im


def solve(c, e, lowest):
    line = sublanes()
    cr, ci, er, ei = c[0], c[1], e[0], e[1]
    good = None
    for k in range(4):
        pivot = jnp.broadcast_to(cr[k : k + 1, 32 * k : 32 * k + 1], TILE)
        floor = jnp.broadcast_to(lowest[k : k + 1, 32 * k : 32 * k + 1], TILE)
        here = pivot > floor
        good = here if good is None else good & here
        inverse = 1.0 / pivot
        rows = [line_of(x, k) * inverse for x in (cr, ci, er, ei)]
        fr, fi = column(cr, k), column(ci, k)
        at = line == k
        cr, ci = (
            jnp.where(at, rows[0], cr - (fr * rows[0] - fi * rows[1])),
            jnp.where(at, rows[1], ci - (fr * rows[1] + fi * rows[0])),
        )
        er, ei = (
            jnp.where(at, rows[2], er - (fr * rows[2] - fi * rows[3])),
            jnp.where(at, rows[3], ei - (fr * rows[3] + fi * rows[2])),
        )
    return (er, ei), good


def add(a, b):
    return a[0] + b[0], a[1] + b[1]


def sub(a, b):
    return a[0] - b[0], a[1] - b[1]


def write_coefficients(out, base, c):
    line, group = sublanes(), group_of_lane()
    for d in range(4):
        here = line == (group + d) % 4
        for part in range(2):
            row = jnp.sum(jnp.where(here, c[part], 0.0), axis=0, keepdims=True)
            out[base + 2 * d + part : base + 2 * d + part + 1, :] = row


def coefficients_body(rows, out, good_out):
    total = jnp.sum(rows[...], axis=0, keepdims=True)
    mu = [read_matrix(total, f) for f in range(4)]
    line, group = sublanes(), group_of_lane()
    diagonal = (line == group) & (line < 4)
    unit = jnp.where(diagonal, 1.0, 0.0)
    alpha, good1 = solve(mu[1], mu[0], PIVOT_GUARD * mu[1][0])
    quad = adjoint_matmul(alpha, matmul(mu[2], alpha))
    right = matmul(mu[1], alpha)
    left = adjoint_matmul(alpha, mu[1])
    rho = add(sub(quad, add(left, right)), mu[0])
    rho_size = jnp.abs(quad[0]) + jnp.abs(left[0]) + jnp.abs(right[0]) + jnp.abs(mu[0][0])
    beta, good0 = solve(mu[0], rho, PIVOT_GUARD * mu[0][0])
    p = (beta[0] + unit, beta[1])
    first = adjoint_matmul(p, matmul(mu[1], p))
    cross = adjoint_matmul(p, matmul(mu[2], alpha))
    cross2 = adjoint_matmul(alpha, matmul(mu[2], p))
    last = adjoint_matmul(alpha, matmul(mu[3], alpha))
    c = add(sub(first, add(cross, cross2)), last)
    c_size = jnp.abs(first[0]) + jnp.abs(cross[0]) + jnp.abs(cross2[0]) + jnp.abs(last[0])
    alpha1, good2 = solve(c, rho, GUARD * c_size)
    _, good3 = solve(rho, unit_pair(unit), GUARD * rho_size)
    q = matmul(alpha, alpha1)
    k = add(alpha, matmul(p, alpha1))
    write_coefficients(out, 0, k)
    write_coefficients(out, 8, q)
    good = good0 & good1 & good2 & good3
    good_out[0] = jnp.min(jnp.where(good, 1, 0))


def unit_pair(unit):
    return unit, jnp.zeros(TILE, F32)


def solve_body(which, c_rows, e_rows, out):
    c = read_matrix(jnp.sum(c_rows[...], axis=0, keepdims=True), which[0])
    e = read_matrix(jnp.sum(e_rows[...], axis=0, keepdims=True), which[1])
    solved, _ = solve(c, e, jnp.zeros(TILE, F32))
    write_coefficients(out, 0, solved)


def mix(re, im, coefficients, base):
    total_re = total_im = None
    for d in range(4):
        x, y = (re, im) if d == 0 else (roll_lanes(re, -32 * d), roll_lanes(im, -32 * d))
        cr = coefficients[base + 2 * d : base + 2 * d + 1, :]
        ci = coefficients[base + 2 * d + 1 : base + 2 * d + 2, :]
        a, b = x * cr - y * ci, x * ci + y * cr
        total_re = a if total_re is None else total_re + a
        total_im = b if total_im is None else total_im + b
    return total_re, total_im


def combine_body(sign, x, y, coefficients, out):
    for t in range(2):
        for c in range(12):
            re, im = mix(y[c, t], y[12 + c, t], coefficients, 0)
            out[c, t] = signed_add(x[c, t], re, sign)
            out[12 + c, t] = signed_add(x[12 + c, t], im, sign)


def final_body(partial, links, *refs):
    recv = in_face_order(refs[:4])
    base, first, image, rows, out = refs[4:]
    for t in range(2):
        b = finished_spinor(partial, links, 0, t, recv, base)
        for s in range(4):
            for c in range(3):
                at = s * 3 + c
                re, im = first[at, t], first[12 + at, t]
                image_re, image_im = image[at, t], image[12 + at, t]
                rk = mix(re, im, rows, 0)
                ak = mix(image_re, image_im, rows, 0)
                aq = mix(image_re, image_im, rows, 8)
                bq = mix(b[0][s][c], b[1][s][c], rows, 8)
                out[pl.ds(2 * at + t, 8, stride=96), :] = rk[0] - aq[0]
                out[pl.ds(2 * (12 + at) + t, 8, stride=96), :] = rk[1] - aq[1]
                out[pl.ds(48 + 2 * at + t, 8, stride=96), :] = re - ak[0] + bq[0]
                out[pl.ds(48 + 2 * (12 + at) + t, 8, stride=96), :] = im - ak[1] + bq[1]


def send_order_body(solution_ref, residual_ref, out):
    for i, ref in enumerate((solution_ref, residual_ref)):
        for c in range(24):
            for t in range(2):
                out[pl.ds(48 * i + 2 * c + t, 8, stride=96), :] = ref[c, t]


def deliver_body(received, solution_ref, residual_ref):
    block_odd = place()[4]
    for i, ref in enumerate((solution_ref, residual_ref)):
        for z in range(2):
            for n in range(6):
                at = 48 * i + 8 * n
                tiles = [received[owner(block_odd, row), z, at : at + 8, :] for row in range(4)]
                for s, tile in enumerate(swap_groups(tiles)):
                    ref[s, pl.ds(16 * n + z, 8, stride=2), :] = tile


SPINOR = (24, 2, 8, 128)
FACES = [(24, 8, 128), (24, 8, 128), (12, 2, 8, 128), (12, 2, 8, 128)]
START_ORDER = (1, 3, 0, 2)


def in_start_order(faces):
    return [faces[i] for i in START_ORDER]


def in_face_order(operands):
    return [operands[START_ORDER.index(i)] for i in range(4)]


def make_pairs(order, start):
    count = len(order)
    out = []
    for i in range(start, start + count, 2):
        a, b = order[i % count], order[(i + 1) % count]
        out += [(a, b), (b, a)]
    return out


def exchange(faces):
    times = list(range(lax.axis_size("ta")))
    blocks = lax.axis_size("gy")
    rows = [gz * blocks + gy for gy in range(blocks) for gz in ROW_OWNER[gy % 2]]
    time_a, time_b, row_a, row_b = faces
    return (
        lax.ppermute(time_a, "ta", make_pairs(times, 0)),
        lax.ppermute(time_b, "ta", make_pairs(times, 1)),
        lax.ppermute(row_a, ("gz", "gy"), make_pairs(rows, 0)),
        lax.ppermute(row_b, ("gz", "gy"), make_pairs(rows, 1)),
    )


def hop_inner(spinor, links, parity, with_moments=False):
    outs = [SPINOR] + ([(5, 8, 128)] if with_moments else [])

    def body(*refs):
        inner_body(parity, with_moments, *refs)

    return call(body, outs, (spinor, links), 8 * 10**6)


def hop_outer(partial, links, recv, parity, base=None, with_faces=True, after=()):
    args = (partial, links, *in_start_order(recv)) + (() if base is None else (base,))

    def body(*refs):
        outer_body(parity, base is not None, with_faces, *refs)

    outs = call(body, [SPINOR] + (FACES if with_faces else []), args, 4 * 10**6, after)
    return outs[0], outs[1:]


def half_normal(spinor, faces, links, with_moments=False, with_faces=True):
    recv = exchange(faces)
    partial, *moments = hop_inner(spinor, links, 1, with_moments)
    odd, faces = hop_outer(partial, links, recv, 1)
    recv = exchange(faces)
    (partial,) = hop_inner(odd, links, 0)
    out, faces = hop_outer(partial, links, recv, 0, spinor, with_faces)
    return out, faces, moments


def faces_only(spinor, links):
    def body(spinor, links, *faces):
        write_faces(spinor, links, 1, faces)

    return call(body, FACES, (spinor, links))


def direct_branch(links, first, image, rows):
    def solve_call(c_rows, e_rows, c_field, e_field):
        def body(*refs):
            solve_body((c_field, e_field), *refs)

        return call(body, [(8, 128)], (c_rows, e_rows), 10**4)[0]

    def combine(sign, x, y, coefficients):
        def body(*refs):
            combine_body(sign, *refs)

        return call(body, [SPINOR], (x, y, coefficients))[0]

    alpha = solve_call(rows, rows, 1, 0)
    residual = combine(-1, first, image, alpha)
    rho = reduce_devices(moments_call(residual, ()))
    beta = solve_call(rows, rho, 0, 0)
    search = combine(1, residual, first, beta)
    faces = faces_only(search, links)
    halfway, faces, _ = half_normal(search, faces, links)
    curvature = reduce_devices(moments_call(halfway, ()))
    images, _, _ = half_normal(halfway, faces, links, with_faces=False)
    alpha1 = solve_call(curvature, rho, 0, 0)
    zero = jnp.zeros(SPINOR, F32)
    solution_field = combine(1, combine(1, zero, first, alpha), search, alpha1)
    residual = combine(-1, residual, images, alpha1)
    return call(send_order_body, [(768, 128)], (solution_field, residual))[0]


def local(sources, gauge_links):
    args = (sources.reshape(4, 96, 128), gauge_links.reshape(4, 144, 128))
    (packed,) = call(pack_body, [(4, 2, 120, 128)], args)
    received = lax.all_to_all(packed, "gz", 0, 0).reshape(960, 128)
    links, first, *faces = call(unpack_body, [(144, 2, 8, 128), SPINOR] + FACES, (received,))
    half1, faces, moments0 = half_normal(first, faces, links, True)
    image, faces, moments1 = half_normal(half1, faces, links, True)
    half2, faces, moments2 = half_normal(image, faces, links, True)

    rows = moments_call(half2, (*moments0, *moments1, *moments2))
    recv = exchange(faces)
    (partial,) = hop_inner(half2, links, 1)
    rows = reduce_rows(rows)
    odd, faces = hop_outer(partial, links, recv, 1, after=(rows,))
    rows = lax.all_to_all(rows, "ta", 0, 0, tiled=True)
    recv = exchange(faces)
    (partial,) = hop_inner(odd, links, 0)
    table, good = call(coefficients_body, [(16, 128)], (rows,), 10**5, flag=True)

    def moment_branch():
        given = (partial, links, *in_start_order(recv), half2, first, image, table)
        return call(final_body, [(768, 128)], given, 10**7)[0]

    out = lax.cond(
        good[0] == 1, moment_branch, lambda: direct_branch(links, first, image, rows)
    )
    received = lax.all_to_all(out.reshape(4, 2, 96, 128), "gz", 0, 0)
    done = call(deliver_body, [(4, 96, 128)] * 2, (received,))
    return tuple(x.reshape(sources.shape) for x in done)


def solution(mesh):
    spinor_spec = P(None, None, None, None, "ta", "gz", "gy")
    link_spec = P(None, None, None, None, None, "ta", "gz", "gy")
    return jax.shard_map(
        local,
        mesh=mesh,
        in_specs=(spinor_spec, link_spec),
        out_specs=(spinor_spec, spinor_spec),
        check_vma=False,
    )
```

```python
import jax
import jax.numpy as jnp
from jax import lax
from jax.experimental import pallas as pl
from jax.experimental.pallas import tpu as pltpu
from jax.sharding import PartitionSpec as P

SRC = 4
KAPPA_SQUARE = 0.0196
GAMMA_COLUMNS = ((3, 2, 1, 0), (3, 2, 1, 0), (2, 3, 0, 1), (2, 3, 0, 1))
GAMMA_PHASES = (
    ((0, 1), (0, 1), (0, -1), (0, -1)),
    ((1, 0), (-1, 0), (-1, 0), (1, 0)),
    ((0, 1), (0, -1), (0, -1), (0, 1)),
    ((1, 0), (1, 0), (1, 0), (1, 0)),
)
F32 = jnp.float32
TILE = (8, 128)
ROW_OWNER = ((0, 1, 3, 2), (2, 3, 1, 0))
GUARD = 0.005
PIVOT_GUARD = 1e-3
VMEM = pl.BlockSpec(memory_space=pltpu.VMEM)
SMEM = pl.BlockSpec(memory_space=pltpu.SMEM)


def call(body, outs, args, flops=10**6, scratch=(), flag=False):
    shapes = [jax.ShapeDtypeStruct(s, F32) for s in outs]
    out_specs = [VMEM] * len(shapes)
    if flag:
        shapes.append(jax.ShapeDtypeStruct((1,), jnp.int32))
        out_specs.append(SMEM)
    moved = 4 * sum(a.size for a in args)
    return pl.pallas_call(
        body,
        out_shape=shapes,
        in_specs=[VMEM] * len(args),
        out_specs=out_specs,
        scratch_shapes=scratch,
        compiler_params=pltpu.CompilerParams(vmem_limit_bytes=16 * 2**20),
        cost_estimate=pl.CostEstimate(flops=flops, bytes_accessed=moved, transcendentals=0),
    )(*args)


def place():
    ta, gz, gy = (lax.axis_index(name) for name in ("ta", "gz", "gy"))
    block_odd = gy % 2
    row_odd = (gz + gz // 2 + block_odd) % 2
    return ta % 2, row_odd, ta == lax.axis_size("ta") - 1, ta == 0, block_odd


def lanes():
    return lax.broadcasted_iota(jnp.int32, TILE, 1)


def sublanes():
    return lax.broadcasted_iota(jnp.int32, TILE, 0)


def roll_lanes(x, shift):
    return pltpu.roll(x, shift % 128, 1)


def swap_groups(tiles):
    low = lanes() < 64
    even = (lanes() // 32) % 2 == 0
    a = [None] * 4
    for i in (0, 1):
        a[i] = jnp.where(low, tiles[i], roll_lanes(tiles[i + 2], 64))
        a[i + 2] = jnp.where(low, roll_lanes(tiles[i], 64), tiles[i + 2])
    out = []
    for i in (0, 2):
        out.append(jnp.where(even, a[i], roll_lanes(a[i + 1], 32)))
        out.append(jnp.where(even, roll_lanes(a[i], -32), a[i + 1]))
    return out


def owner(block_odd, row):
    return jnp.where(block_odd == 1, ROW_OWNER[1][row], ROW_OWNER[0][row])


def pack_body(sources, links, out):
    block_odd = place()[4]
    for ref, base, chunks in ((sources, 0, 6), (links, 48, 9)):
        for z in range(2):
            for i in range(chunks):
                tiles = [ref[s, pl.ds(16 * i + z, 8, stride=2), :] for s in range(4)]
                for row, tile in enumerate(swap_groups(tiles)):
                    out[owner(block_odd, row), z, base + 8 * i : base + 8 * i + 8, :] = tile


def unpack_body(received, links, spinor, *faces):
    for c in range(24):
        for t in range(2):
            spinor[c, t] = received[pl.ds(2 * c + t, 8, stride=120), :]
    low = lanes() < 64
    even = (lanes() // 32) % 2 == 0
    for l in range(36):
        for t in range(2):
            x = received[pl.ds(48 + 2 * l + t, 8, stride=120), :]
            half = roll_lanes(x, 64)
            for q, pair in ((0, jnp.where(low, x, half)), (2, jnp.where(low, half, x))):
                turned = roll_lanes(pair, 32)
                links[q * 36 + l, t] = jnp.where(even, pair, turned)
                links[(q + 1) * 36 + l, t] = jnp.where(even, turned, pair)
    write_faces(spinor, links, 1, faces)


def load_spinor(ref, t):
    return [[[ref[(p * 4 + s) * 3 + c, t] for c in range(3)] for s in range(4)] for p in range(2)]


def signed_add(a, b, sign):
    return a + b if sign > 0 else a - b


def turn(phase, part):
    if phase[1] == 0:
        return part, phase[0]
    return 1 - part, -phase[1] if part == 0 else phase[1]


def project(v, direction, hop):
    out = [[None, None], [None, None]]
    for part in range(2):
        for k in range(2):
            partner = GAMMA_COLUMNS[direction][k]
            other, sign = turn(GAMMA_PHASES[direction][k], part)
            out[part][k] = [
                signed_add(v[part][k][c], v[other][partner][c], sign * hop) for c in range(3)
            ]
    return out


def rebuild_add(acc, half, direction, hop):
    for part in range(2):
        for s in range(4):
            if s < 2:
                source, sign = half[part][s], 1
            else:
                other, sign = turn(GAMMA_PHASES[direction][s], part)
                source, sign = half[other][GAMMA_COLUMNS[direction][s]], sign * hop
            for c in range(3):
                old = acc[part][s][c]
                if old is None:
                    acc[part][s][c] = source[c] if sign > 0 else -source[c]
                else:
                    acc[part][s][c] = signed_add(old, source[c], sign)


def color_times(links, parity, direction, t, half, adjoint):
    base = (parity * 4 + direction) * 18
    out = [[[None] * 3 for _ in range(2)] for _ in range(2)]
    for row in range(3):
        for column in range(3):
            entry = 3 * column + row if adjoint else 3 * row + column
            re, im = links[base + entry, t], links[base + 9 + entry, t]
            for k in range(2):
                x, y = half[0][k][column], half[1][k][column]
                if adjoint:
                    a, b = re * x + im * y, re * y - im * x
                else:
                    a, b = re * x - im * y, re * y + im * x
                if out[0][k][row] is None:
                    out[0][k][row], out[1][k][row] = a, b
                else:
                    out[0][k][row] += a
                    out[1][k][row] += b
    return out


def map_half(f, half):
    return [[[f(x) for x in row] for row in part] for part in half]


def halves(half):
    return [half[p][k][c] for p in range(2) for k in range(2) for c in range(3)]


def write_faces(spinor, links, parity, faces):
    time_a, time_b, row_a, row_b = faces
    time_odd, row_odd = (flag == 1 for flag in place()[:2])
    for t in range(2):
        v = load_spinor(spinor, t)
        down = halves(project(v, 1, -1))
        up = halves(color_times(links, 1 - parity, 1, t, project(v, 1, 1), True))
        for i in range(12):
            row_a[i, t] = jnp.where(row_odd, down[i], up[i])
            row_b[i, t] = jnp.where(row_odd, up[i], down[i])
        if t == 0:
            time_down = halves(project(v, 3, -1))
        else:
            time_up = halves(color_times(links, 1 - parity, 3, t, project(v, 3, 1), True))
    for i in range(12):
        time_a[i] = jnp.where(time_odd, time_down[i], time_up[i])
        time_b[i] = jnp.where(time_odd, time_up[i], time_down[i])


def inner_body(parity, with_moments, spinor, links, out, *moments):
    cell = lanes() % 32
    site = sublanes() + place()[1] + parity
    vs = [load_spinor(spinor, t) for t in range(2)]
    for t in range(2):
        odd = (site + t) % 2 == 1
        v = vs[t]
        acc = [[[None] * 3 for _ in range(4)] for _ in range(2)]

        def next_cell(x):
            moved = jnp.where(cell == 31, roll_lanes(x, 31), roll_lanes(x, -1))
            return jnp.where(odd, moved, x)

        def prior_cell(x):
            moved = jnp.where(cell == 0, roll_lanes(x, -31), roll_lanes(x, 1))
            return jnp.where(odd, x, moved)

        half = map_half(next_cell, project(v, 0, -1))
        rebuild_add(acc, color_times(links, parity, 0, t, half, False), 0, -1)
        half = color_times(links, 1 - parity, 0, t, project(v, 0, 1), True)
        rebuild_add(acc, map_half(prior_cell, half), 0, 1)
        half = map_half(lambda x: pltpu.roll(x, 7, 0), project(v, 2, -1))
        rebuild_add(acc, color_times(links, parity, 2, t, half, False), 2, -1)
        half = color_times(links, 1 - parity, 2, t, project(v, 2, 1), True)
        rebuild_add(acc, map_half(lambda x: pltpu.roll(x, 1, 0), half), 2, 1)
        if t == 0:
            half = project(vs[1], 3, -1)
            rebuild_add(acc, color_times(links, parity, 3, 0, half, False), 3, -1)
        else:
            half = color_times(links, 1 - parity, 3, 0, project(vs[0], 3, 1), True)
            rebuild_add(acc, half, 3, 1)
        for p in range(2):
            for s in range(4):
                for c in range(3):
                    out[(p * 4 + s) * 3 + c, t] = acc[p][s][c]
    if with_moments:
        for i, total in enumerate(moment_tiles(spinor)):
            moments[0][i] = total


def moment_tiles(spinor):
    totals = [jnp.zeros(TILE, F32) for _ in range(5)]
    for t in range(2):
        for c in range(12):
            re, im = spinor[c, t], spinor[12 + c, t]
            totals[0] = totals[0] + (re * re + im * im)
            for d in (1, 2):
                re_d, im_d = roll_lanes(re, -32 * d), roll_lanes(im, -32 * d)
                totals[2 * d - 1] = totals[2 * d - 1] + (re * re_d + im * im_d)
                totals[2 * d] = totals[2 * d] + (re * im_d - im * re_d)
    return totals


def add_received(acc, links, parity, t, recv):
    time_a, time_b, row_a, row_b = recv
    time_odd, row_odd, last, first, _ = place()
    time_odd, row_odd = time_odd == 1, row_odd == 1

    def pick(flag, first, second):
        flat = [jnp.where(flag, first[i], second[i]) for i in range(12)]
        return [[flat[6 * p + 3 * k : 6 * p + 3 * k + 3] for k in range(2)] for p in range(2)]

    half = pick(row_odd, [row_b[i, t] for i in range(12)], [row_a[i, t] for i in range(12)])
    rebuild_add(acc, color_times(links, parity, 1, t, half, False), 1, -1)
    half = pick(row_odd, [row_a[i, t] for i in range(12)], [row_b[i, t] for i in range(12)])
    rebuild_add(acc, half, 1, 1)
    a, b = [time_a[i] for i in range(12)], [time_b[i] for i in range(12)]
    if t == 1:
        sign = jnp.where(last, -1.0, 1.0)
        half = map_half(lambda x: x * sign, pick(time_odd, b, a))
        rebuild_add(acc, color_times(links, parity, 3, t, half, False), 3, -1)
    else:
        sign = jnp.where(first, -1.0, 1.0)
        half = map_half(lambda x: x * sign, pick(time_odd, a, b))
        rebuild_add(acc, half, 3, 1)


def finished_spinor(partial, links, parity, t, recv, base):
    acc = load_spinor(partial, t)
    add_received(acc, links, parity, t, recv)
    if base is None:
        return acc
    old = load_spinor(base, t)
    for p in range(2):
        for s in range(4):
            for c in range(3):
                hopped = KAPPA_SQUARE * acc[p][s][c]
                acc[p][s][c] = old[p][s][c] - hopped if s < 2 else hopped - old[p][s][c]
    return acc


def outer_body(parity, base, partial, links, recv, out, faces):
    recv = in_face_order(recv)
    for t in range(2):
        acc = finished_spinor(partial, links, parity, t, recv, base)
        for p in range(2):
            for s in range(4):
                for c in range(3):
                    out[(p * 4 + s) * 3 + c, t] = acc[p][s][c]
    if faces:
        write_faces(out, links, 1 - parity, faces)


def group_sum(x):
    cell = lax.broadcasted_iota(jnp.int32, x.shape, 1) % 32
    for step in (16, 8, 4, 2, 1):
        x = x + jnp.where(cell < 32 - step, roll_lanes(x, -step), roll_lanes(x, 32 - step))
    return x


def pick_cells(scratch, out):
    rows = group_sum(scratch[...])
    cell = lax.broadcasted_iota(jnp.int32, rows.shape, 1) % 32
    line = lax.broadcasted_iota(jnp.int32, rows.shape, 0)
    packed = jnp.sum(jnp.where(cell == line, rows, 0.0), axis=0, keepdims=True)
    out[...] = jnp.broadcast_to(packed[None], out.shape)


def moments_body(spinor, given, out, scratch):
    scratch[...] = jnp.zeros(scratch.shape, F32)
    at = 0
    for total in [[m[i] for i in range(5)] for m in given] + [moment_tiles(spinor)]:
        for tile in total:
            scratch[at : at + 1, :] = jnp.sum(tile, axis=0, keepdims=True)
            at += 1
    pick_cells(scratch, out)


MOMENT_SCRATCH = [pltpu.VMEM((24, 128), F32)]


def moments_call(spinor):
    def body(spinor, out, scratch):
        moments_body(spinor, (), out, scratch)

    return call(body, [(32, 8, 128)], (spinor,), 10**5, scratch=MOMENT_SCRATCH)[0]


def row_sum_body(rows, out):
    total = jnp.sum(rows[:, 0, :], axis=0, keepdims=True)
    out[...] = jnp.broadcast_to(total[None], out.shape)


def reduce_rows(rows):
    rows = lax.all_to_all(rows, ("gz", "gy"), 0, 0, tiled=True)
    return call(row_sum_body, [(16, 16, 128)], (rows,), 10**4)[0]


def reduce_devices(rows):
    return lax.all_to_all(reduce_rows(rows), "ta", 0, 0, tiled=True)


def group_of_lane():
    return lanes() // 32


def read_matrix(total, field):
    line, group = sublanes(), group_of_lane()
    re, im = jnp.zeros(TILE, F32), jnp.zeros(TILE, F32)

    def value(q, g):
        lane = 32 * g + 5 * field + q
        return jnp.broadcast_to(total[:, lane : lane + 1], TILE)

    for i in range(4):
        re = jnp.where((line == i) & (group == i), value(0, i), re)
        for d in (1, 2):
            if d == 2 and i >= 2:
                continue
            j = (i + d) % 4
            x, y = value(2 * d - 1, i), value(2 * d, i)
            here, there = (line == i) & (group == j), (line == j) & (group == i)
            re = jnp.where(here | there, x, re)
            im = jnp.where(here, y, jnp.where(there, -y, im))
    return re, im


def column(x, k):
    return jnp.broadcast_to(x[:, 32 * k : 32 * k + 1], TILE)


def line_of(x, k):
    return jnp.broadcast_to(x[k : k + 1, :], TILE)


def matmul(a, b):
    re, im = jnp.zeros(TILE, F32), jnp.zeros(TILE, F32)
    for k in range(4):
        ar, ai, br, bi = column(a[0], k), column(a[1], k), line_of(b[0], k), line_of(b[1], k)
        re = re + (ar * br - ai * bi)
        im = im + (ar * bi + ai * br)
    return re, im


def adjoint_matmul(a, b):
    line, group = sublanes(), group_of_lane()
    re, im = jnp.zeros(TILE, F32), jnp.zeros(TILE, F32)
    for k in range(4):
        ar, ai = jnp.zeros(TILE, F32), jnp.zeros(TILE, F32)
        for i in range(4):
            here = line == i
            ar = jnp.where(here, jnp.broadcast_to(a[0][k : k + 1, 32 * i : 32 * i + 1], TILE), ar)
            ai = jnp.where(here, jnp.broadcast_to(a[1][k : k + 1, 32 * i : 32 * i + 1], TILE), ai)
        br, bi = line_of(b[0], k), line_of(b[1], k)
        re = re + (ar * br + ai * bi)
        im = im + (ar * bi - ai * br)
    return re, im


def solve(c, e, lowest):
    line = sublanes()
    cr, ci, er, ei = c[0], c[1], e[0], e[1]
    good = None
    for k in range(4):
        pivot = jnp.broadcast_to(cr[k : k + 1, 32 * k : 32 * k + 1], TILE)
        floor = jnp.broadcast_to(lowest[k : k + 1, 32 * k : 32 * k + 1], TILE)
        here = pivot > floor
        good = here if good is None else good & here
        inverse = 1.0 / pivot
        rows = [line_of(x, k) * inverse for x in (cr, ci, er, ei)]
        fr, fi = column(cr, k), column(ci, k)
        at = line == k
        cr, ci = (
            jnp.where(at, rows[0], cr - (fr * rows[0] - fi * rows[1])),
            jnp.where(at, rows[1], ci - (fr * rows[1] + fi * rows[0])),
        )
        er, ei = (
            jnp.where(at, rows[2], er - (fr * rows[2] - fi * rows[3])),
            jnp.where(at, rows[3], ei - (fr * rows[3] + fi * rows[2])),
        )
    return (er, ei), good


def add(a, b):
    return a[0] + b[0], a[1] + b[1]


def sub(a, b):
    return a[0] - b[0], a[1] - b[1]


def write_coefficients(out, base, c):
    line, group = sublanes(), group_of_lane()
    for d in range(4):
        here = line == (group + d) % 4
        for part in range(2):
            row = jnp.sum(jnp.where(here, c[part], 0.0), axis=0, keepdims=True)
            out[base + 2 * d + part : base + 2 * d + part + 1, :] = row


def coefficients_body(rows, out, good_out):
    total = jnp.sum(rows[:, 0, :], axis=0, keepdims=True)
    mu = [read_matrix(total, f) for f in range(4)]
    line, group = sublanes(), group_of_lane()
    diagonal = (line == group) & (line < 4)
    unit = jnp.where(diagonal, 1.0, 0.0)
    alpha, good1 = solve(mu[1], mu[0], PIVOT_GUARD * mu[1][0])
    quad = adjoint_matmul(alpha, matmul(mu[2], alpha))
    right = matmul(mu[1], alpha)
    left = adjoint_matmul(alpha, mu[1])
    rho = add(sub(quad, add(left, right)), mu[0])
    rho_size = jnp.abs(quad[0]) + jnp.abs(left[0]) + jnp.abs(right[0]) + jnp.abs(mu[0][0])
    beta, good0 = solve(mu[0], rho, PIVOT_GUARD * mu[0][0])
    p = (beta[0] + unit, beta[1])
    first = adjoint_matmul(p, matmul(mu[1], p))
    cross = adjoint_matmul(p, matmul(mu[2], alpha))
    cross2 = adjoint_matmul(alpha, matmul(mu[2], p))
    last = adjoint_matmul(alpha, matmul(mu[3], alpha))
    c = add(sub(first, add(cross, cross2)), last)
    c_size = jnp.abs(first[0]) + jnp.abs(cross[0]) + jnp.abs(cross2[0]) + jnp.abs(last[0])
    alpha1, good2 = solve(c, rho, GUARD * c_size)
    _, good3 = solve(rho, unit_pair(unit), GUARD * rho_size)
    q = matmul(alpha, alpha1)
    k = add(alpha, matmul(p, alpha1))
    write_coefficients(out, 0, k)
    write_coefficients(out, 8, q)
    good = good0 & good1 & good2 & good3
    good_out[0] = jnp.min(jnp.where(good, 1, 0))


def unit_pair(unit):
    return unit, jnp.zeros(TILE, F32)


def solve_body(which, c_rows, e_rows, out):
    c = read_matrix(jnp.sum(c_rows[:, 0, :], axis=0, keepdims=True), which[0])
    e = read_matrix(jnp.sum(e_rows[:, 0, :], axis=0, keepdims=True), which[1])
    solved, _ = solve(c, e, jnp.zeros(TILE, F32))
    write_coefficients(out, 0, solved)


def mix(re, im, coefficients, base):
    total_re = total_im = None
    for d in range(4):
        x, y = (re, im) if d == 0 else (roll_lanes(re, -32 * d), roll_lanes(im, -32 * d))
        cr = coefficients[base + 2 * d : base + 2 * d + 1, :]
        ci = coefficients[base + 2 * d + 1 : base + 2 * d + 2, :]
        a, b = x * cr - y * ci, x * ci + y * cr
        total_re = a if total_re is None else total_re + a
        total_im = b if total_im is None else total_im + b
    return total_re, total_im


def combine_body(sign, x, y, coefficients, out):
    for t in range(2):
        for c in range(12):
            re, im = mix(y[c, t], y[12 + c, t], coefficients, 0)
            out[c, t] = signed_add(x[c, t], re, sign)
            out[12 + c, t] = signed_add(x[12 + c, t], im, sign)


def final_body(partial, links, *refs):
    recv = in_face_order(refs[:4])
    base, first, image, rows, out = refs[4:]
    for t in range(2):
        b = finished_spinor(partial, links, 0, t, recv, base)
        for s in range(4):
            for c in range(3):
                at = s * 3 + c
                re, im = first[at, t], first[12 + at, t]
                image_re, image_im = image[at, t], image[12 + at, t]
                rk = mix(re, im, rows, 0)
                ak = mix(image_re, image_im, rows, 0)
                aq = mix(image_re, image_im, rows, 8)
                bq = mix(b[0][s][c], b[1][s][c], rows, 8)
                out[pl.ds(2 * at + t, 8, stride=96), :] = rk[0] - aq[0]
                out[pl.ds(2 * (12 + at) + t, 8, stride=96), :] = rk[1] - aq[1]
                out[pl.ds(48 + 2 * at + t, 8, stride=96), :] = re - ak[0] + bq[0]
                out[pl.ds(48 + 2 * (12 + at) + t, 8, stride=96), :] = im - ak[1] + bq[1]


def send_order_body(solution_ref, residual_ref, out):
    for i, ref in enumerate((solution_ref, residual_ref)):
        for c in range(24):
            for t in range(2):
                out[pl.ds(48 * i + 2 * c + t, 8, stride=96), :] = ref[c, t]


def deliver_body(received, solution_ref, residual_ref):
    block_odd = place()[4]
    for i, ref in enumerate((solution_ref, residual_ref)):
        for z in range(2):
            for n in range(6):
                at = 48 * i + 8 * n
                tiles = [received[owner(block_odd, row), z, at : at + 8, :] for row in range(4)]
                for s, tile in enumerate(swap_groups(tiles)):
                    ref[s, pl.ds(16 * n + z, 8, stride=2), :] = tile


SPINOR = (24, 2, 8, 128)
FACES = [(24, 8, 128), (24, 8, 128), (12, 2, 8, 128), (12, 2, 8, 128)]
START_ORDER = (1, 3, 0, 2)


def in_start_order(faces):
    return [faces[i] for i in START_ORDER]


def in_face_order(operands):
    return [operands[START_ORDER.index(i)] for i in range(4)]


def make_pairs(order, start):
    count = len(order)
    out = []
    for i in range(start, start + count, 2):
        a, b = order[i % count], order[(i + 1) % count]
        out += [(a, b), (b, a)]
    return out


def exchange(faces):
    times = list(range(lax.axis_size("ta")))
    blocks = lax.axis_size("gy")
    rows = [gz * blocks + gy for gy in range(blocks) for gz in ROW_OWNER[gy % 2]]
    time_a, time_b, row_a, row_b = faces
    return (
        lax.ppermute(time_a, "ta", make_pairs(times, 0)),
        lax.ppermute(time_b, "ta", make_pairs(times, 1)),
        lax.ppermute(row_a, ("gz", "gy"), make_pairs(rows, 0)),
        lax.ppermute(row_b, ("gz", "gy"), make_pairs(rows, 1)),
    )


def hop_inner(spinor, links, parity, with_moments=False):
    outs = [SPINOR] + ([(5, 8, 128)] if with_moments else [])

    def body(*refs):
        inner_body(parity, with_moments, *refs)

    return call(body, outs, (spinor, links), 8 * 10**6)


def hop_outer(partial, links, recv, parity, base=None, with_faces=True, moments=(), rows=None):
    outs = [SPINOR] + (FACES if with_faces else [])
    args = (partial, links, *in_start_order(recv))
    extra = moments if rows is None else (rows,)
    if base is not None:
        args += (base,)
    used, made = len(args), len(outs)

    def body(*refs):
        given, results = refs[: used + len(extra)], refs[used + len(extra) :]
        old = None if base is None else given[6]
        outer_body(parity, old, given[0], given[1], given[2:6], results[0], results[1:made])
        if moments:
            moments_body(results[0], given[used:], results[made], results[-1])
        if rows is not None:
            row_sum_body(given[used], results[made])

    scratch = MOMENT_SCRATCH if moments else ()
    more = [(32, 8, 128)] if moments else [] if rows is None else [(16, 16, 128)]
    results = call(body, outs + more, args + tuple(extra), 4 * 10**6, scratch)
    return results[0], results[1:made], results[made:]


def half_normal(spinor, faces, links, with_moments=False, with_faces=True, moments=()):
    recv = exchange(faces)
    partial, *made = hop_inner(spinor, links, 1, with_moments)
    odd, faces, _ = hop_outer(partial, links, recv, 1)
    recv = exchange(faces)
    (partial,) = hop_inner(odd, links, 0)
    if moments:
        moments = (*moments, *made)
    out, faces, rows = hop_outer(partial, links, recv, 0, spinor, with_faces, moments)
    return out, faces, rows or made


def faces_only(spinor, links):
    def body(spinor, links, *faces):
        write_faces(spinor, links, 1, faces)

    return call(body, FACES, (spinor, links))


def direct_branch(links, first, image, rows):
    def solve_call(c_rows, e_rows, c_field, e_field):
        def body(*refs):
            solve_body((c_field, e_field), *refs)

        return call(body, [(8, 128)], (c_rows, e_rows), 10**4)[0]

    def combine(sign, x, y, coefficients):
        def body(*refs):
            combine_body(sign, *refs)

        return call(body, [SPINOR], (x, y, coefficients))[0]

    alpha = solve_call(rows, rows, 1, 0)
    residual = combine(-1, first, image, alpha)
    rho = reduce_devices(moments_call(residual))
    beta = solve_call(rows, rho, 0, 0)
    search = combine(1, residual, first, beta)
    faces = faces_only(search, links)
    halfway, faces, _ = half_normal(search, faces, links)
    curvature = reduce_devices(moments_call(halfway))
    images, _, _ = half_normal(halfway, faces, links, with_faces=False)
    alpha1 = solve_call(curvature, rho, 0, 0)
    zero = jnp.zeros(SPINOR, F32)
    solution_field = combine(1, combine(1, zero, first, alpha), search, alpha1)
    residual = combine(-1, residual, images, alpha1)
    return call(send_order_body, [(768, 128)], (solution_field, residual))[0]


def local(sources, gauge_links):
    args = (sources.reshape(4, 96, 128), gauge_links.reshape(4, 144, 128))
    (packed,) = call(pack_body, [(4, 2, 120, 128)], args)
    received = lax.all_to_all(packed, "gz", 0, 0).reshape(960, 128)
    links, first, *faces = call(unpack_body, [(144, 2, 8, 128), SPINOR] + FACES, (received,))
    half1, faces, moments0 = half_normal(first, faces, links, True)
    image, faces, moments1 = half_normal(half1, faces, links, True)
    half2, faces, (rows,) = half_normal(
        image, faces, links, True, moments=(*moments0, *moments1)
    )

    rows = lax.all_to_all(rows, ("gz", "gy"), 0, 0, tiled=True)
    recv = exchange(faces)
    (partial,) = hop_inner(half2, links, 1)
    odd, faces, (rows,) = hop_outer(partial, links, recv, 1, rows=rows)
    rows = lax.all_to_all(rows, "ta", 0, 0, tiled=True)
    recv = exchange(faces)
    (partial,) = hop_inner(odd, links, 0)
    table, good = call(coefficients_body, [(16, 128)], (rows,), 10**5, flag=True)

    def moment_branch():
        given = (partial, links, *in_start_order(recv), half2, first, image, table)
        return call(final_body, [(768, 128)], given, 10**7)[0]

    out = lax.cond(
        good[0] == 1, moment_branch, lambda: direct_branch(links, first, image, rows)
    )
    received = lax.all_to_all(out.reshape(4, 2, 96, 128), "gz", 0, 0)
    done = call(deliver_body, [(4, 96, 128)] * 2, (received,))
    return tuple(x.reshape(sources.shape) for x in done)


def solution(mesh):
    spinor_spec = P(None, None, None, None, "ta", "gz", "gy")
    link_spec = P(None, None, None, None, None, "ta", "gz", "gy")
    return jax.shard_map(
        local,
        mesh=mesh,
        in_specs=(spinor_spec, link_spec),
        out_specs=(spinor_spec, spinor_spec),
        check_vma=False,
    )
```

```python
import jax
import jax.numpy as jnp
from jax import lax
from jax.experimental import pallas as pl
from jax.experimental.pallas import tpu as pltpu
from jax.sharding import PartitionSpec as P

SRC = 4
KAPPA_SQUARE = 0.0196
GAMMA_COLUMNS = ((3, 2, 1, 0), (3, 2, 1, 0), (2, 3, 0, 1), (2, 3, 0, 1))
GAMMA_PHASES = (
    ((0, 1), (0, 1), (0, -1), (0, -1)),
    ((1, 0), (-1, 0), (-1, 0), (1, 0)),
    ((0, 1), (0, -1), (0, -1), (0, 1)),
    ((1, 0), (1, 0), (1, 0), (1, 0)),
)
F32 = jnp.float32
TILE = (8, 128)
ROW_OWNER = ((0, 1, 3, 2), (2, 3, 1, 0))
GUARD = 0.005
PIVOT_GUARD = 1e-3
VMEM = pl.BlockSpec(memory_space=pltpu.VMEM)
SMEM = pl.BlockSpec(memory_space=pltpu.SMEM)
HBM = pl.BlockSpec(memory_space=pltpu.HBM)


def call(body, outs, args, flops=10**6, scratch=(), flag=False, inputs=VMEM):
    shapes = [jax.ShapeDtypeStruct(s, F32) for s in outs]
    out_specs = [VMEM] * len(shapes)
    if flag:
        shapes.append(jax.ShapeDtypeStruct((1,), jnp.int32))
        out_specs.append(SMEM)
    moved = 4 * sum(a.size for a in args)
    return pl.pallas_call(
        body,
        out_shape=shapes,
        in_specs=[inputs] * len(args),
        out_specs=out_specs,
        scratch_shapes=scratch,
        compiler_params=pltpu.CompilerParams(vmem_limit_bytes=16 * 2**20),
        cost_estimate=pl.CostEstimate(flops=flops, bytes_accessed=moved, transcendentals=0),
    )(*args)


def place():
    ta, gz, gy = (lax.axis_index(name) for name in ("ta", "gz", "gy"))
    block_odd = gy % 2
    row_odd = (gz + gz // 2 + block_odd) % 2
    return ta % 2, row_odd, ta == lax.axis_size("ta") - 1, ta == 0, block_odd


def lanes():
    return lax.broadcasted_iota(jnp.int32, TILE, 1)


def sublanes():
    return lax.broadcasted_iota(jnp.int32, TILE, 0)


def roll_lanes(x, shift):
    return pltpu.roll(x, shift % 128, 1)


def swap_groups(tiles):
    low = lanes() < 64
    even = (lanes() // 32) % 2 == 0
    a = [None] * 4
    for i in (0, 1):
        a[i] = jnp.where(low, tiles[i], roll_lanes(tiles[i + 2], 64))
        a[i + 2] = jnp.where(low, roll_lanes(tiles[i], 64), tiles[i + 2])
    out = []
    for i in (0, 2):
        out.append(jnp.where(even, a[i], roll_lanes(a[i + 1], 32)))
        out.append(jnp.where(even, roll_lanes(a[i], -32), a[i + 1]))
    return out


def owner(block_odd, row):
    return jnp.where(block_odd == 1, ROW_OWNER[1][row], ROW_OWNER[0][row])


def pack_body(sources, links, out, sources_here, links_here, done):
    block_odd = place()[4]
    copies = [
        pltpu.make_async_copy(sources, sources_here, done.at[0]),
        pltpu.make_async_copy(links, links_here, done.at[1]),
    ]
    for copy in copies:
        copy.start()
    parts = ((sources_here, 0, 6), (links_here, 48, 9))
    for copy, (ref, base, chunks) in zip(copies, parts):
        copy.wait()
        for z in range(2):
            for i in range(chunks):
                tiles = [ref[s, pl.ds(16 * i + z, 8, stride=2), :] for s in range(4)]
                for row, tile in enumerate(swap_groups(tiles)):
                    out[owner(block_odd, row), z, base + 8 * i : base + 8 * i + 8, :] = tile


def unpack_body(received, links, spinor, *faces):
    for c in range(24):
        for t in range(2):
            spinor[c, t] = received[pl.ds(2 * c + t, 8, stride=120), :]
    low = lanes() < 64
    even = (lanes() // 32) % 2 == 0
    for l in range(36):
        for t in range(2):
            x = received[pl.ds(48 + 2 * l + t, 8, stride=120), :]
            half = roll_lanes(x, 64)
            for q, pair in ((0, jnp.where(low, x, half)), (2, jnp.where(low, half, x))):
                turned = roll_lanes(pair, 32)
                links[q * 36 + l, t] = jnp.where(even, pair, turned)
                links[(q + 1) * 36 + l, t] = jnp.where(even, turned, pair)
    write_faces(spinor, links, 1, faces)


def load_spinor(ref, t):
    return [[[ref[(p * 4 + s) * 3 + c, t] for c in range(3)] for s in range(4)] for p in range(2)]


def signed_add(a, b, sign):
    return a + b if sign > 0 else a - b


def turn(phase, part):
    if phase[1] == 0:
        return part, phase[0]
    return 1 - part, -phase[1] if part == 0 else phase[1]


def project(v, direction, hop):
    out = [[None, None], [None, None]]
    for part in range(2):
        for k in range(2):
            partner = GAMMA_COLUMNS[direction][k]
            other, sign = turn(GAMMA_PHASES[direction][k], part)
            out[part][k] = [
                signed_add(v[part][k][c], v[other][partner][c], sign * hop) for c in range(3)
            ]
    return out


def rebuild_add(acc, half, direction, hop):
    for part in range(2):
        for s in range(4):
            if s < 2:
                source, sign = half[part][s], 1
            else:
                other, sign = turn(GAMMA_PHASES[direction][s], part)
                source, sign = half[other][GAMMA_COLUMNS[direction][s]], sign * hop
            for c in range(3):
                old = acc[part][s][c]
                if old is None:
                    acc[part][s][c] = source[c] if sign > 0 else -source[c]
                else:
                    acc[part][s][c] = signed_add(old, source[c], sign)


def color_times(links, parity, direction, t, half, adjoint):
    base = (parity * 4 + direction) * 18
    out = [[[None] * 3 for _ in range(2)] for _ in range(2)]
    for row in range(3):
        for column in range(3):
            entry = 3 * column + row if adjoint else 3 * row + column
            re, im = links[base + entry, t], links[base + 9 + entry, t]
            for k in range(2):
                x, y = half[0][k][column], half[1][k][column]
                if adjoint:
                    a, b = re * x + im * y, re * y - im * x
                else:
                    a, b = re * x - im * y, re * y + im * x
                if out[0][k][row] is None:
                    out[0][k][row], out[1][k][row] = a, b
                else:
                    out[0][k][row] += a
                    out[1][k][row] += b
    return out


def map_half(f, half):
    return [[[f(x) for x in row] for row in part] for part in half]


def halves(half):
    return [half[p][k][c] for p in range(2) for k in range(2) for c in range(3)]


def write_faces(spinor, links, parity, faces):
    time_a, time_b, row_a, row_b = faces
    time_odd, row_odd = (flag == 1 for flag in place()[:2])
    for t in range(2):
        v = load_spinor(spinor, t)
        down = halves(project(v, 1, -1))
        up = halves(color_times(links, 1 - parity, 1, t, project(v, 1, 1), True))
        for i in range(12):
            row_a[i, t] = jnp.where(row_odd, down[i], up[i])
            row_b[i, t] = jnp.where(row_odd, up[i], down[i])
        if t == 0:
            time_down = halves(project(v, 3, -1))
        else:
            time_up = halves(color_times(links, 1 - parity, 3, t, project(v, 3, 1), True))
    for i in range(12):
        time_a[i] = jnp.where(time_odd, time_down[i], time_up[i])
        time_b[i] = jnp.where(time_odd, time_up[i], time_down[i])


def inner_body(parity, with_moments, spinor, links, out, *moments):
    cell = lanes() % 32
    site = sublanes() + place()[1] + parity
    vs = [load_spinor(spinor, t) for t in range(2)]
    for t in range(2):
        odd = (site + t) % 2 == 1
        v = vs[t]
        acc = [[[None] * 3 for _ in range(4)] for _ in range(2)]

        def next_cell(x):
            moved = jnp.where(cell == 31, roll_lanes(x, 31), roll_lanes(x, -1))
            return jnp.where(odd, moved, x)

        def prior_cell(x):
            moved = jnp.where(cell == 0, roll_lanes(x, -31), roll_lanes(x, 1))
            return jnp.where(odd, x, moved)

        half = map_half(next_cell, project(v, 0, -1))
        rebuild_add(acc, color_times(links, parity, 0, t, half, False), 0, -1)
        half = color_times(links, 1 - parity, 0, t, project(v, 0, 1), True)
        rebuild_add(acc, map_half(prior_cell, half), 0, 1)
        half = map_half(lambda x: pltpu.roll(x, 7, 0), project(v, 2, -1))
        rebuild_add(acc, color_times(links, parity, 2, t, half, False), 2, -1)
        half = color_times(links, 1 - parity, 2, t, project(v, 2, 1), True)
        rebuild_add(acc, map_half(lambda x: pltpu.roll(x, 1, 0), half), 2, 1)
        if t == 0:
            half = project(vs[1], 3, -1)
            rebuild_add(acc, color_times(links, parity, 3, 0, half, False), 3, -1)
        else:
            half = color_times(links, 1 - parity, 3, 0, project(vs[0], 3, 1), True)
            rebuild_add(acc, half, 3, 1)
        for p in range(2):
            for s in range(4):
                for c in range(3):
                    out[(p * 4 + s) * 3 + c, t] = acc[p][s][c]
    if with_moments:
        for i, total in enumerate(moment_tiles(spinor)):
            moments[0][i] = total


def moment_tiles(spinor):
    totals = [jnp.zeros(TILE, F32) for _ in range(5)]
    for t in range(2):
        for c in range(12):
            re, im = spinor[c, t], spinor[12 + c, t]
            totals[0] = totals[0] + (re * re + im * im)
            for d in (1, 2):
                re_d, im_d = roll_lanes(re, -32 * d), roll_lanes(im, -32 * d)
                totals[2 * d - 1] = totals[2 * d - 1] + (re * re_d + im * im_d)
                totals[2 * d] = totals[2 * d] + (re * im_d - im * re_d)
    return totals


def add_received(acc, links, parity, t, recv):
    time_a, time_b, row_a, row_b = recv
    time_odd, row_odd, last, first, _ = place()
    time_odd, row_odd = time_odd == 1, row_odd == 1

    def pick(flag, first, second):
        flat = [jnp.where(flag, first[i], second[i]) for i in range(12)]
        return [[flat[6 * p + 3 * k : 6 * p + 3 * k + 3] for k in range(2)] for p in range(2)]

    half = pick(row_odd, [row_b[i, t] for i in range(12)], [row_a[i, t] for i in range(12)])
    rebuild_add(acc, color_times(links, parity, 1, t, half, False), 1, -1)
    half = pick(row_odd, [row_a[i, t] for i in range(12)], [row_b[i, t] for i in range(12)])
    rebuild_add(acc, half, 1, 1)
    a, b = [time_a[i] for i in range(12)], [time_b[i] for i in range(12)]
    if t == 1:
        sign = jnp.where(last, -1.0, 1.0)
        half = map_half(lambda x: x * sign, pick(time_odd, b, a))
        rebuild_add(acc, color_times(links, parity, 3, t, half, False), 3, -1)
    else:
        sign = jnp.where(first, -1.0, 1.0)
        half = map_half(lambda x: x * sign, pick(time_odd, a, b))
        rebuild_add(acc, half, 3, 1)


def finished_spinor(partial, links, parity, t, recv, base):
    acc = load_spinor(partial, t)
    add_received(acc, links, parity, t, recv)
    if base is None:
        return acc
    old = load_spinor(base, t)
    for p in range(2):
        for s in range(4):
            for c in range(3):
                hopped = KAPPA_SQUARE * acc[p][s][c]
                acc[p][s][c] = old[p][s][c] - hopped if s < 2 else hopped - old[p][s][c]
    return acc


def outer_body(parity, base, partial, links, recv, out, faces):
    recv = in_face_order(recv)
    for t in range(2):
        acc = finished_spinor(partial, links, parity, t, recv, base)
        for p in range(2):
            for s in range(4):
                for c in range(3):
                    out[(p * 4 + s) * 3 + c, t] = acc[p][s][c]
    if faces:
        write_faces(out, links, 1 - parity, faces)


def group_sum(x):
    cell = lax.broadcasted_iota(jnp.int32, x.shape, 1) % 32
    for step in (16, 8, 4, 2, 1):
        x = x + jnp.where(cell < 32 - step, roll_lanes(x, -step), roll_lanes(x, 32 - step))
    return x


def pick_cells(scratch, out):
    rows = group_sum(scratch[...])
    cell = lax.broadcasted_iota(jnp.int32, rows.shape, 1) % 32
    line = lax.broadcasted_iota(jnp.int32, rows.shape, 0)
    packed = jnp.sum(jnp.where(cell == line, rows, 0.0), axis=0, keepdims=True)
    out[...] = jnp.broadcast_to(packed[None], out.shape)


def moments_body(spinor, given, out, scratch):
    scratch[...] = jnp.zeros(scratch.shape, F32)
    at = 0
    for total in [[m[i] for i in range(5)] for m in given] + [moment_tiles(spinor)]:
        for tile in total:
            scratch[at : at + 1, :] = jnp.sum(tile, axis=0, keepdims=True)
            at += 1
    pick_cells(scratch, out)


MOMENT_SCRATCH = [pltpu.VMEM((24, 128), F32)]


def moments_call(spinor):
    def body(spinor, out, scratch):
        moments_body(spinor, (), out, scratch)

    return call(body, [(32, 8, 128)], (spinor,), 10**5, scratch=MOMENT_SCRATCH)[0]


def row_sum_body(rows, out):
    total = jnp.sum(rows[:, 0, :], axis=0, keepdims=True)
    out[...] = jnp.broadcast_to(total[None], out.shape)


def reduce_rows(rows):
    rows = lax.all_to_all(rows, ("gz", "gy"), 0, 0, tiled=True)
    return call(row_sum_body, [(16, 16, 128)], (rows,), 10**4)[0]


def reduce_devices(rows):
    return lax.all_to_all(reduce_rows(rows), "ta", 0, 0, tiled=True)


def group_of_lane():
    return lanes() // 32


def read_matrix(total, field):
    line, group = sublanes(), group_of_lane()
    re, im = jnp.zeros(TILE, F32), jnp.zeros(TILE, F32)

    def value(q, g):
        lane = 32 * g + 5 * field + q
        return jnp.broadcast_to(total[:, lane : lane + 1], TILE)

    for i in range(4):
        re = jnp.where((line == i) & (group == i), value(0, i), re)
        for d in (1, 2):
            if d == 2 and i >= 2:
                continue
            j = (i + d) % 4
            x, y = value(2 * d - 1, i), value(2 * d, i)
            here, there = (line == i) & (group == j), (line == j) & (group == i)
            re = jnp.where(here | there, x, re)
            im = jnp.where(here, y, jnp.where(there, -y, im))
    return re, im


def column(x, k):
    return jnp.broadcast_to(x[:, 32 * k : 32 * k + 1], TILE)


def line_of(x, k):
    return jnp.broadcast_to(x[k : k + 1, :], TILE)


def matmul(a, b):
    re, im = jnp.zeros(TILE, F32), jnp.zeros(TILE, F32)
    for k in range(4):
        ar, ai, br, bi = column(a[0], k), column(a[1], k), line_of(b[0], k), line_of(b[1], k)
        re = re + (ar * br - ai * bi)
        im = im + (ar * bi + ai * br)
    return re, im


def adjoint_matmul(a, b):
    line, group = sublanes(), group_of_lane()
    re, im = jnp.zeros(TILE, F32), jnp.zeros(TILE, F32)
    for k in range(4):
        ar, ai = jnp.zeros(TILE, F32), jnp.zeros(TILE, F32)
        for i in range(4):
            here = line == i
            ar = jnp.where(here, jnp.broadcast_to(a[0][k : k + 1, 32 * i : 32 * i + 1], TILE), ar)
            ai = jnp.where(here, jnp.broadcast_to(a[1][k : k + 1, 32 * i : 32 * i + 1], TILE), ai)
        br, bi = line_of(b[0], k), line_of(b[1], k)
        re = re + (ar * br + ai * bi)
        im = im + (ar * bi - ai * br)
    return re, im


def solve(c, e, lowest):
    line = sublanes()
    cr, ci, er, ei = c[0], c[1], e[0], e[1]
    good = None
    for k in range(4):
        pivot = jnp.broadcast_to(cr[k : k + 1, 32 * k : 32 * k + 1], TILE)
        floor = jnp.broadcast_to(lowest[k : k + 1, 32 * k : 32 * k + 1], TILE)
        here = pivot > floor
        good = here if good is None else good & here
        inverse = 1.0 / pivot
        rows = [line_of(x, k) * inverse for x in (cr, ci, er, ei)]
        fr, fi = column(cr, k), column(ci, k)
        at = line == k
        cr, ci = (
            jnp.where(at, rows[0], cr - (fr * rows[0] - fi * rows[1])),
            jnp.where(at, rows[1], ci - (fr * rows[1] + fi * rows[0])),
        )
        er, ei = (
            jnp.where(at, rows[2], er - (fr * rows[2] - fi * rows[3])),
            jnp.where(at, rows[3], ei - (fr * rows[3] + fi * rows[2])),
        )
    return (er, ei), good


def add(a, b):
    return a[0] + b[0], a[1] + b[1]


def sub(a, b):
    return a[0] - b[0], a[1] - b[1]


def write_coefficients(out, base, c):
    line, group = sublanes(), group_of_lane()
    for d in range(4):
        here = line == (group + d) % 4
        for part in range(2):
            row = jnp.sum(jnp.where(here, c[part], 0.0), axis=0, keepdims=True)
            out[base + 2 * d + part : base + 2 * d + part + 1, :] = row


def write_table(out, base, c):
    group = group_of_lane()
    for part in range(2):
        for j in range(4):
            x = jnp.where(group == j, c[part], 0.0)
            x = x + roll_lanes(x, 64)
            out[base + 4 * part + j] = x + roll_lanes(x, 32)


def coefficients_body(rows, out, good_out):
    total = jnp.sum(rows[:, 0, :], axis=0, keepdims=True)
    mu = [read_matrix(total, f) for f in range(4)]
    line, group = sublanes(), group_of_lane()
    diagonal = (line == group) & (line < 4)
    unit = jnp.where(diagonal, 1.0, 0.0)
    alpha, good1 = solve(mu[1], mu[0], PIVOT_GUARD * mu[1][0])
    quad = adjoint_matmul(alpha, matmul(mu[2], alpha))
    right = matmul(mu[1], alpha)
    left = adjoint_matmul(alpha, mu[1])
    rho = add(sub(quad, add(left, right)), mu[0])
    rho_size = jnp.abs(quad[0]) + jnp.abs(left[0]) + jnp.abs(right[0]) + jnp.abs(mu[0][0])
    beta, good0 = solve(mu[0], rho, PIVOT_GUARD * mu[0][0])
    p = (beta[0] + unit, beta[1])
    first = adjoint_matmul(p, matmul(mu[1], p))
    cross = adjoint_matmul(p, matmul(mu[2], alpha))
    cross2 = adjoint_matmul(alpha, matmul(mu[2], p))
    last = adjoint_matmul(alpha, matmul(mu[3], alpha))
    c = add(sub(first, add(cross, cross2)), last)
    c_size = jnp.abs(first[0]) + jnp.abs(cross[0]) + jnp.abs(cross2[0]) + jnp.abs(last[0])
    alpha1, good2 = solve(c, rho, GUARD * c_size)
    _, good3 = solve(rho, unit_pair(unit), GUARD * rho_size)
    q = matmul(alpha, alpha1)
    k = add(alpha, matmul(p, alpha1))
    write_table(out, 0, k)
    write_table(out, 8, q)
    good = good0 & good1 & good2 & good3
    good_out[0] = jnp.min(jnp.where(good, 1, 0))


def unit_pair(unit):
    return unit, jnp.zeros(TILE, F32)


def solve_body(which, c_rows, e_rows, out):
    c = read_matrix(jnp.sum(c_rows[:, 0, :], axis=0, keepdims=True), which[0])
    e = read_matrix(jnp.sum(e_rows[:, 0, :], axis=0, keepdims=True), which[1])
    solved, _ = solve(c, e, jnp.zeros(TILE, F32))
    write_coefficients(out, 0, solved)


def mix(re, im, coefficients, base):
    total_re = total_im = None
    for d in range(4):
        x, y = (re, im) if d == 0 else (roll_lanes(re, -32 * d), roll_lanes(im, -32 * d))
        cr = coefficients[base + 2 * d : base + 2 * d + 1, :]
        ci = coefficients[base + 2 * d + 1 : base + 2 * d + 2, :]
        a, b = x * cr - y * ci, x * ci + y * cr
        total_re = a if total_re is None else total_re + a
        total_im = b if total_im is None else total_im + b
    return total_re, total_im


def combine_body(sign, x, y, coefficients, out):
    for t in range(2):
        for c in range(12):
            re, im = mix(y[c, t], y[12 + c, t], coefficients, 0)
            out[c, t] = signed_add(x[c, t], re, sign)
            out[12 + c, t] = signed_add(x[12 + c, t], im, sign)


def send_body(partial, links, *refs):
    recv = in_face_order(refs[:4])
    base, image, out = refs[4:]
    for t in range(2):
        for c in range(24):
            out[pl.ds(2 * c + t, 8, stride=96), :] = image[c, t]
        b = finished_spinor(partial, links, 0, t, recv, base)
        for p in range(2):
            for s in range(4):
                for c in range(3):
                    at = (p * 4 + s) * 3 + c
                    out[pl.ds(48 + 2 * at + t, 8, stride=96), :] = b[p][s][c]


def returned(received, block_odd, z, at):
    return swap_groups([received[owner(block_odd, r), z, at : at + 8, :] for r in range(4)])


def weighted(total, re, im, table, base, j, sign):
    for i in range(4):
        cr = table[base + j, i : i + 1, :]
        ci = table[base + 4 + j, i : i + 1, :]
        real, imag = re[i] * cr - im[i] * ci, re[i] * ci + im[i] * cr
        if total is None:
            total = (real, imag)
        else:
            total = (signed_add(total[0], real, sign), signed_add(total[1], imag, sign))
    return total


def final_body(sources, received, table, solution_ref, residual_ref):
    block_odd = place()[4]
    for z in range(2):
        for n in range(3):
            rows = [pl.ds(16 * (n + 3 * part) + z, 8, stride=2) for part in range(2)]
            r = [[sources[s, rows[part], :] for s in range(4)] for part in range(2)]
            a = [returned(received, block_odd, z, 8 * (n + 3 * part)) for part in range(2)]
            b = [returned(received, block_odd, z, 48 + 8 * (n + 3 * part)) for part in range(2)]
            for j in range(4):
                x = weighted(None, r[0], r[1], table, 0, j, 1)
                x = weighted(x, a[0], a[1], table, 8, j, -1)
                y = weighted((r[0][j], r[1][j]), a[0], a[1], table, 0, j, -1)
                y = weighted(y, b[0], b[1], table, 8, j, 1)
                for part in range(2):
                    solution_ref[j, rows[part], :] = x[part]
                    residual_ref[j, rows[part], :] = y[part]


def send_order_body(solution_ref, residual_ref, out):
    for i, ref in enumerate((solution_ref, residual_ref)):
        for c in range(24):
            for t in range(2):
                out[pl.ds(48 * i + 2 * c + t, 8, stride=96), :] = ref[c, t]


def deliver_body(received, solution_ref, residual_ref):
    block_odd = place()[4]
    for i, ref in enumerate((solution_ref, residual_ref)):
        for z in range(2):
            for n in range(6):
                for s, tile in enumerate(returned(received, block_odd, z, 48 * i + 8 * n)):
                    ref[s, pl.ds(16 * n + z, 8, stride=2), :] = tile


SPINOR = (24, 2, 8, 128)
ORIGINAL = (4, 96, 128)
FACES = [(24, 8, 128), (24, 8, 128), (12, 2, 8, 128), (12, 2, 8, 128)]
START_ORDER = (3, 1, 0, 2)


def in_start_order(faces):
    return [faces[i] for i in START_ORDER]


def in_face_order(operands):
    return [operands[START_ORDER.index(i)] for i in range(4)]


def make_pairs(order, start):
    count = len(order)
    out = []
    for i in range(start, start + count, 2):
        a, b = order[i % count], order[(i + 1) % count]
        out += [(a, b), (b, a)]
    return out


def exchange(faces):
    times = list(range(lax.axis_size("ta")))
    blocks = lax.axis_size("gy")
    rows = [gz * blocks + gy for gy in range(blocks) for gz in ROW_OWNER[gy % 2]]
    time_a, time_b, row_a, row_b = faces
    return (
        lax.ppermute(time_a, "ta", make_pairs(times, 0)),
        lax.ppermute(time_b, "ta", make_pairs(times, 1)),
        lax.ppermute(row_a, ("gz", "gy"), make_pairs(rows, 0)),
        lax.ppermute(row_b, ("gz", "gy"), make_pairs(rows, 1)),
    )


def hop_inner(spinor, links, parity, with_moments=False):
    outs = [SPINOR] + ([(5, 8, 128)] if with_moments else [])

    def body(*refs):
        inner_body(parity, with_moments, *refs)

    return call(body, outs, (spinor, links), 8 * 10**6)


def hop_outer(partial, links, recv, parity, base=None, with_faces=True, moments=(), rows=None):
    outs = [SPINOR] + (FACES if with_faces else [])
    args = (partial, links, *in_start_order(recv))
    extra = moments if rows is None else (rows,)
    if base is not None:
        args += (base,)
    used, made = len(args), len(outs)

    def body(*refs):
        given, results = refs[: used + len(extra)], refs[used + len(extra) :]
        old = None if base is None else given[6]
        outer_body(parity, old, given[0], given[1], given[2:6], results[0], results[1:made])
        if moments:
            moments_body(results[0], given[used:], results[made], results[-1])
        if rows is not None:
            row_sum_body(given[used], results[made])

    scratch = MOMENT_SCRATCH if moments else ()
    more = [(32, 8, 128)] if moments else [] if rows is None else [(16, 16, 128)]
    results = call(body, outs + more, args + tuple(extra), 4 * 10**6, scratch)
    return results[0], results[1:made], results[made:]


def half_normal(spinor, faces, links, with_moments=False, with_faces=True, moments=()):
    recv = exchange(faces)
    partial, *made = hop_inner(spinor, links, 1, with_moments)
    odd, faces, _ = hop_outer(partial, links, recv, 1)
    recv = exchange(faces)
    (partial,) = hop_inner(odd, links, 0)
    if moments:
        moments = (*moments, *made)
    out, faces, rows = hop_outer(partial, links, recv, 0, spinor, with_faces, moments)
    return out, faces, rows or made


def faces_only(spinor, links):
    def body(spinor, links, *faces):
        write_faces(spinor, links, 1, faces)

    return call(body, FACES, (spinor, links))


def give_back(out):
    return lax.all_to_all(out.reshape(4, 2, 96, 128), "gz", 0, 0)


def direct_branch(links, first, image, rows):
    def solve_call(c_rows, e_rows, c_field, e_field):
        def body(*refs):
            solve_body((c_field, e_field), *refs)

        return call(body, [(8, 128)], (c_rows, e_rows), 10**4)[0]

    def combine(sign, x, y, coefficients):
        def body(*refs):
            combine_body(sign, *refs)

        return call(body, [SPINOR], (x, y, coefficients))[0]

    alpha = solve_call(rows, rows, 1, 0)
    residual = combine(-1, first, image, alpha)
    rho = reduce_devices(moments_call(residual))
    beta = solve_call(rows, rho, 0, 0)
    search = combine(1, residual, first, beta)
    faces = faces_only(search, links)
    halfway, faces, _ = half_normal(search, faces, links)
    curvature = reduce_devices(moments_call(halfway))
    images, _, _ = half_normal(halfway, faces, links, with_faces=False)
    alpha1 = solve_call(curvature, rho, 0, 0)
    zero = jnp.zeros(SPINOR, F32)
    solution_field = combine(1, combine(1, zero, first, alpha), search, alpha1)
    residual = combine(-1, residual, images, alpha1)
    (out,) = call(send_order_body, [(768, 128)], (solution_field, residual))
    return tuple(call(deliver_body, [ORIGINAL] * 2, (give_back(out),)))


def local(sources, gauge_links):
    flat = sources.reshape(ORIGINAL)
    here = [pltpu.VMEM(ORIGINAL, F32), pltpu.VMEM((4, 144, 128), F32), pltpu.SemaphoreType.DMA((2,))]
    args = (flat, gauge_links.reshape(4, 144, 128))
    (packed,) = call(pack_body, [(4, 2, 120, 128)], args, scratch=here, inputs=HBM)
    received = lax.all_to_all(packed, "gz", 0, 0).reshape(960, 128)
    links, first, *faces = call(unpack_body, [(144, 2, 8, 128), SPINOR] + FACES, (received,))
    half1, faces, moments0 = half_normal(first, faces, links, True)
    image, faces, moments1 = half_normal(half1, faces, links, True)
    half2, faces, (rows,) = half_normal(
        image, faces, links, True, moments=(*moments0, *moments1)
    )

    rows = lax.all_to_all(rows, ("gz", "gy"), 0, 0, tiled=True)
    recv = exchange(faces)
    (partial,) = hop_inner(half2, links, 1)
    odd, faces, (rows,) = hop_outer(partial, links, recv, 1, rows=rows)
    rows = lax.all_to_all(rows, "ta", 0, 0, tiled=True)
    recv = exchange(faces)
    (partial,) = hop_inner(odd, links, 0)
    given = (partial, links, *in_start_order(recv), half2, image)
    received = give_back(call(send_body, [(768, 128)], given, 10**7)[0])
    table, good = call(coefficients_body, [(16, 8, 128)], (rows,), 10**5, flag=True)
    done = lax.cond(
        good[0] == 1,
        lambda: tuple(call(final_body, [ORIGINAL] * 2, (flat, received, table))),
        lambda: direct_branch(links, first, image, rows),
    )
    return tuple(x.reshape(sources.shape) for x in done)


def solution(mesh):
    spinor_spec = P(None, None, None, None, "ta", "gz", "gy")
    link_spec = P(None, None, None, None, None, "ta", "gz", "gy")
    return jax.shard_map(
        local,
        mesh=mesh,
        in_specs=(spinor_spec, link_spec),
        out_specs=(spinor_spec, spinor_spec),
        check_vma=False,
    )
```
